512 devices in a mesh: gx: 8 (over y, core), gy: 4 (over x), gz: 16 (over z).
Axes of the slice: x: 4, y: 4, z: 16, core: 2. Of those that a mesh axis runs over, the one named last changes fastest.
Arguments:
- right_side: float32 [40, 8, 4, 8192], P(None, 'gx', 'gy', 'gz'), may hold values from -16 to 16
- elem_faces: int32 [4, 8, 4, 4096], P(None, 'gx', 'gy', 'gz'), may hold values from 0 to 895
- elem_class: int32 [8, 4, 4096], P('gx', 'gy', 'gz'), may hold values from 0 to 1
- elem_scale: float32 [8, 4, 4096], P('gx', 'gy', 'gz'), may hold values from 0.5 to 2
- stretch: float32 [3, 8, 4, 4096], P(None, 'gx', 'gy', 'gz'), may hold values from 0.25 to 4
- pml_flag: int32 [8, 4, 4096], P('gx', 'gy', 'gz'), may hold values from 0 to 1, as said below
- send_faces: int32 [6, 8, 4, 1024], P(None, 'gx', 'gy', 'gz'), may hold values from 0 to 511, as said below
- blocks: float32 [2, 3, 2, 6400], replicated, may hold values from -0.5 to 0.5
Outputs:
- solution_field: float32 [40, 8, 4, 8192], P(None, 'gx', 'gy', 'gz')
- residual: float32 [40, 8, 4, 8192], P(None, 'gx', 'gy', 'gz')
The draws below stay inside these ranges and needn't reach their ends.
Inputs may be any that keep to these rules, and one draw needn't show every extreme that they name: `pml_flag`: on a device at position k along gz, with n devices along gz, h = n // 2 and t = min(k, n - 1 - k), exactly 64 * (h - 1 - t) // (h - 1) elements are flagged; devices at positions k and k + h together hold at most 64. `send_faces`: the 384 entries of one device are different faces.
All inputs are finite; a program needn't handle non-finite values.
Results may differ from the reference program's by a relative error of at most 0.0003.
Values sent between devices are 32-bit elements; how exact they have to be, the bound alone decides.
A program may use at most 128 MiB of HBM per device.

```python
import math
import jax
import jax.numpy as jnp
from jax import lax

DOF = 20
NREF = 2
ITERS = 4
FACE_DEV = 512
BORDER = 64
ELEM_DEV = 256
PML_MAX = 64
N_GX = 8
N_GY = 4
N_GZ = 16


def device_keys(base_key, count):
    return jax.vmap(lambda number: jax.random.fold_in(base_key, number))(jnp.arange(count, dtype=jnp.int32))


def draw_right_side(key, part):
    key = jax.random.fold_in(key, 11)
    devices = N_GX * N_GY * N_GZ
    shape = (2 * DOF, N_GX, N_GY, N_GZ * FACE_DEV)
    first = jnp.arange(N_GX, dtype=jnp.int32)[:, None, None]
    second = jnp.arange(N_GY, dtype=jnp.int32)[None, :, None]
    third = (jnp.arange(N_GZ * FACE_DEV, dtype=jnp.int32) // FACE_DEV)[None, None, :]
    linear = ((first * N_GY + second) * N_GZ + third).astype(jnp.float32)
    ramp = 1.0 + 2.0 * linear / (devices - 1)
    values = jnp.clip(jax.random.normal(key, shape, jnp.float32), -4.0, 4.0)
    return (values * ramp[None]).astype(jnp.float32)


def draw_pml_flag(key, part):
    key = jax.random.fold_in(key, 23)
    keys = device_keys(key, N_GX * N_GY * N_GZ)
    orders = jax.vmap(lambda single: jax.random.permutation(single, ELEM_DEV))(keys)
    orders = orders.astype(jnp.int32).reshape(N_GX, N_GY, N_GZ, ELEM_DEV)
    position = jnp.arange(N_GZ, dtype=jnp.int32)
    nearest = jnp.minimum(position, N_GZ - 1 - position)
    half_count = N_GZ // 2
    counts = PML_MAX * (half_count - 1 - nearest) // (half_count - 1)
    marked = (orders < counts[None, None, :, None]).astype(jnp.int32)
    return marked.reshape(N_GX, N_GY, N_GZ * ELEM_DEV)


def draw_send_faces(key, part):
    key = jax.random.fold_in(key, 37)
    keys = device_keys(key, N_GX * N_GY * N_GZ)
    orders = jax.vmap(lambda single: jax.random.permutation(single, FACE_DEV)[:6 * BORDER])(keys)
    orders = orders.astype(jnp.int32).reshape(N_GX, N_GY, N_GZ, 6, BORDER).transpose(3, 0, 1, 2, 4)
    return orders.reshape(6, N_GX, N_GY, N_GZ * BORDER)


def touch_ends(values, own_key, least, high):
    spot = [jax.random.randint(jax.random.fold_in(own_key, axis), (), 0, length) for axis, length in enumerate(values.shape)]
    longest = values.shape.index(max(values.shape))
    next_to = spot[:longest] + [(spot[longest] + 1) % values.shape[longest]] + spot[longest + 1:]
    return values.at[tuple(spot)].set(least).at[tuple(next_to)].set(high)


def block_scale(own_key, shape, shards, least, high):
    def one(axis_at, parts):
        draws = jax.random.uniform(jax.random.fold_in(jax.random.fold_in(own_key, 6), axis_at), (parts,), jnp.float32, least / len(shards), high / len(shards))
        return jnp.repeat(jnp.exp(draws), shape[axis_at] // parts).reshape((-1,) + (1,) * (len(shape) - axis_at - 1))

    gain = one(*shards[0])
    for cut in shards[1:]:
        gain = gain * one(*cut)
    return gain


def gaussian(own_key, extent, width, limit, kind=jnp.bfloat16):
    return jnp.clip(width * jax.random.normal(own_key, extent, jnp.float32), -limit, limit).astype(kind)


def setup_inputs(seed: int = 0) -> dict:
    arg_keys = jax.random.split(jax.random.key(seed), 9)
    right_side = draw_right_side(jax.random.fold_in(arg_keys[8], 71), 0)
    elem_faces = touch_ends(jax.random.randint(arg_keys[1], (4, N_GX, N_GY, N_GZ * ELEM_DEV), 0, FACE_DEV + 6 * BORDER), jax.random.fold_in(arg_keys[1], 1), 0, (FACE_DEV + 6 * BORDER) - 1).astype(jnp.int32)
    elem_class = touch_ends(jax.random.randint(arg_keys[2], (N_GX, N_GY, N_GZ * ELEM_DEV), 0, NREF), jax.random.fold_in(arg_keys[2], 1), 0, NREF - 1).astype(jnp.int32)
    elem_scale = jnp.clip(jnp.exp(math.log(2.0) - 1.3862944 * jax.random.uniform(arg_keys[3], (N_GX, N_GY, N_GZ * ELEM_DEV), jnp.float32) ** block_scale(arg_keys[3], (N_GX, N_GY, N_GZ * ELEM_DEV), ((0, 8), (1, 4), (2, 16)), -0.2, 0.2)), 0.5, 2.0)
    stretch = jnp.clip(jnp.exp(math.log(4.0) - 2.7725887 * jax.random.uniform(arg_keys[4], (3, N_GX, N_GY, N_GZ * ELEM_DEV), jnp.float32) ** block_scale(arg_keys[4], (3, N_GX, N_GY, N_GZ * ELEM_DEV), ((1, 8), (2, 4), (3, 16)), -0.2, 0.2)), 0.25, 4.0)
    pml_flag = draw_pml_flag(jax.random.fold_in(arg_keys[8], 71), 0)
    send_faces = draw_send_faces(jax.random.fold_in(arg_keys[8], 71), 0)
    blocks = gaussian(arg_keys[7], (NREF, 3, 2, 16 * DOF * DOF), (8 * DOF) ** -0.5, 0.5, jnp.float32)
    return dict(right_side=right_side, elem_faces=elem_faces, elem_class=elem_class, elem_scale=elem_scale, stretch=stretch, pml_flag=pml_flag, send_faces=send_faces, blocks=blocks)


SIGMA = 1.0
HIGHEST = lax.Precision.HIGHEST


def real_split(blocks):
    classes = blocks.shape[0]
    unknowns = DOF
    real_part = blocks[:, :, 0].reshape(classes, 3, 4, unknowns, 4, unknowns)
    imag_part = blocks[:, :, 1].reshape(classes, 3, 4, unknowns, 4, unknowns)
    upper_row = jnp.stack([real_part, -imag_part], axis=5)
    lower_row = jnp.stack([imag_part, real_part], axis=5)
    joined = jnp.stack([upper_row, lower_row], axis=3)
    joined = joined.transpose(0, 1, 3, 4, 2, 6, 7, 5)
    return joined.reshape(classes * 3, 8 * unknowns, 8 * unknowns)


def from_lower(portion, grid_axis):
    padding = jnp.zeros_like(lax.slice_in_dim(portion, 0, 1, axis=grid_axis))
    kept = lax.slice_in_dim(portion, 0, portion.shape[grid_axis] - 1, axis=grid_axis)
    return jnp.concatenate([padding, kept], axis=grid_axis)


def from_upper(portion, grid_axis):
    padding = jnp.zeros_like(lax.slice_in_dim(portion, 0, 1, axis=grid_axis))
    kept = lax.slice_in_dim(portion, 1, portion.shape[grid_axis], axis=grid_axis)
    return jnp.concatenate([kept, padding], axis=grid_axis)


def trade_all(stacked):
    pieces = []
    for grid_axis in range(3):
        pieces.append(from_lower(stacked[:, :, :, :, 2 * grid_axis + 1], grid_axis))
        pieces.append(from_upper(stacked[:, :, :, :, 2 * grid_axis], grid_axis))
    return jnp.stack(pieces, axis=4)


def local_terms(extended, elem_map, member_class, scaling, stretch_rows, marked, gram_blocks, real_blocks):
    elements = elem_map.shape[1]
    trace_width = extended.shape[0]
    gathered = extended[:, elem_map].reshape(4 * trace_width, elements)
    onehot = (member_class[None, :] == jnp.arange(NREF, dtype=jnp.int32)[:, None]).astype(jnp.float32)
    base_coef = onehot * scaling[None, :]
    products = jnp.einsum("rij,je->rie", gram_blocks, gathered, precision=HIGHEST)
    result = jnp.sum(products * base_coef[:, None, :], axis=0)
    running = jnp.cumsum(marked, dtype=jnp.int32)
    position = jnp.where(marked > 0, running - 1, PML_MAX)
    pml_rows = jnp.zeros((PML_MAX,), jnp.int32).at[position].set(jnp.arange(elements, dtype=jnp.int32), mode="drop")
    occupied = jnp.zeros((PML_MAX,), jnp.float32).at[position].set(1.0, mode="drop")
    stretch_coef = (onehot[:, None, :] * (scaling[None, :] * (stretch_rows - 1.0))[None]).reshape(NREF * 3, elements)
    pml_weight = stretch_coef[:, pml_rows] * occupied[None, :]
    projected = jnp.einsum("kij,js->kis", real_blocks, gathered[:, pml_rows], precision=HIGHEST) * pml_weight[:, None, :]
    pml_terms = jnp.einsum("kji,kjs->is", real_blocks, projected, precision=HIGHEST)
    result = result.at[:, pml_rows].add(pml_terms * occupied[None, :])
    spread = jnp.zeros(extended.shape, jnp.float32)
    return spread.at[:, elem_map].add(result.reshape(trace_width, 4, elements))


def to_grid(source_array, leading, trailing):
    shaped = source_array.reshape(leading, N_GX, N_GY, N_GZ, trailing)
    return shaped.transpose(1, 2, 3, 0, 4)


def reference(right_side, elem_faces, elem_class, elem_scale, stretch, pml_flag, send_faces, blocks):
    trace_width = 2 * DOF
    devices = N_GX * N_GY * N_GZ
    source = to_grid(right_side, trace_width, FACE_DEV).reshape(devices, trace_width, FACE_DEV)
    elem_map = to_grid(elem_faces, 4, ELEM_DEV).reshape(devices, 4, ELEM_DEV)
    member_class = elem_class.reshape(devices, ELEM_DEV)
    scaling = elem_scale.reshape(devices, ELEM_DEV)
    stretch_rows = to_grid(stretch, 3, ELEM_DEV).reshape(devices, 3, ELEM_DEV)
    marked = pml_flag.reshape(devices, ELEM_DEV)
    border_faces = to_grid(send_faces, 6, BORDER).reshape(devices, 6, BORDER)
    real_blocks = real_split(blocks)
    split_four = real_blocks.reshape(NREF, 3, real_blocks.shape[1], real_blocks.shape[2])
    gram_blocks = jnp.einsum("rdji,rdjk->rik", split_four, split_four, precision=HIGHEST)

    def pick_rows(vector, linked):
        return vector[:, linked]

    def add_rows(vector, linked, addend):
        return vector.at[:, linked].add(addend)

    def device_terms(packed):
        return local_terms(packed[0], packed[1], packed[2], packed[3], packed[4], packed[5], gram_blocks, real_blocks)

    def operate(vector):
        outgoing = jax.vmap(pick_rows)(vector, border_faces)
        incoming = trade_all(outgoing.reshape(N_GX, N_GY, N_GZ, trace_width, 6, BORDER))
        incoming = incoming.reshape(devices, trace_width, 6 * BORDER)
        extended = jnp.concatenate([vector, incoming], axis=2)
        spread = lax.map(device_terms, (extended, elem_map, member_class, scaling, stretch_rows, marked))
        owned_part = spread[:, :, :FACE_DEV]
        back_part = spread[:, :, FACE_DEV:].reshape(N_GX, N_GY, N_GZ, trace_width, 6, BORDER)
        returned = trade_all(back_part).reshape(devices, trace_width, 6, BORDER)
        owned_part = jax.vmap(add_rows)(owned_part, border_faces, returned)
        return SIGMA * vector + owned_part

    solution = jnp.zeros_like(source)
    residual = source
    direction = source
    norm_now = jnp.sum(residual * residual)
    for iteration in range(ITERS):
        applied = operate(direction)
        step_size = norm_now / jnp.sum(direction * applied)
        solution = solution + step_size * direction
        residual = residual - step_size * applied
        norm_next = jnp.sum(residual * residual)
        direction = residual + (norm_next / norm_now) * direction
        norm_now = norm_next

    def to_output(field_array):
        shaped = field_array.reshape(N_GX, N_GY, N_GZ, trace_width, FACE_DEV).transpose(3, 0, 1, 2, 4)
        return shaped.reshape(trace_width, N_GX, N_GY, N_GZ * FACE_DEV)

    return to_output(solution), to_output(residual)
```

```python
import functools

import jax
import jax.numpy as jnp
import numpy as np
from jax import lax
from jax.experimental import pallas as pl
from jax.experimental.pallas import tpu as pltpu
from jax.sharding import PartitionSpec as P

MESH = pl.DeviceIdType.MESH
F32 = jnp.float32
BF16 = jnp.bfloat16
N_GX, N_GY, N_GZ = 8, 4, 16
AXES = (("gx", N_GX), ("gy", N_GY), ("gz", N_GZ))
PLANE = N_GX * N_GY
THETA = 4096.0
SHIFT = 1.75
LANES = 128


def dot(a, b):
    return jnp.dot(a, b, preferred_element_type=F32)


def dot_nt(a, b):
    return lax.dot_general(a, b, (((1,), (1,)), ((), ())), preferred_element_type=F32)


def pieces(value, count):
    out = []
    for _ in range(count):
        head = value.astype(BF16).astype(F32)
        out.append(head)
        value = value - head
    return out


def onehot(left, right):
    return jnp.where(left == right, 1.0, 0.0).astype(BF16)


def embed_matrix():
    out = np.zeros((256, 1024), np.float32)
    for j in range(80):
        face, unknown = divmod(j, 20)
        for part in range(2):
            column = 512 * part + 40 * face + 20 * part + unknown
            out[j, column] = 1.0
            out[j, column + 160] = 1.0
            out[128 + j, column + 320] = 1.0
    return out


def kernel(
    rhs_ref,
    faces_ref,
    class_ref,
    scale_ref,
    stretch_ref,
    flag_ref,
    send_ref,
    blocks_ref,
    embed_ref,
    sol_ref,
    res_ref,
    place,
    pick,
    raw,
    smat,
    smat_t,
    rows,
    zhi,
    zlo,
    part,
    inbox,
    plane_buf,
    line_buf,
    halo_send,
    halo_recv,
    plane_send,
    plane_recv,
    line_send,
    line_recv,
):
    at = {name: lax.axis_index(name) for name, _ in AXES}
    size = dict(AXES)

    def device(**moved):
        return tuple(moved.get(name, at[name]) for name, _ in AXES)

    neighbours, exists = [], []
    for name, n in AXES:
        neighbours.append(device(**{name: lax.rem(at[name] + (n - 1), n)}))
        neighbours.append(device(**{name: lax.rem(at[name] + 1, n)}))
        exists.append(at[name] > 0)
        exists.append(at[name] < n - 1)
    plane_at = at["gx"] * N_GY + at["gy"]
    plane_devices = []
    for step in range(1, PLANE):
        other = lax.rem(plane_at + step, PLANE)
        plane_devices.append(device(gx=other // N_GY, gy=lax.rem(other, N_GY)))
    line_devices = []
    for step in sorted(range(1, N_GZ), key=lambda d: -min(d, N_GZ - d)):
        line_devices.append(device(gz=lax.rem(at["gz"] + step, N_GZ)))

    barrier = pltpu.get_barrier_semaphore()
    for other in plane_devices + line_devices:
        pl.semaphore_signal(barrier, inc=1, device_id=other, device_id_type=MESH)

    sends = []

    def send_halo(step):
        for k in range(6):
            copy = pltpu.make_async_remote_copy(
                src_ref=part.at[step, k],
                dst_ref=inbox.at[step, k ^ 1],
                send_sem=halo_send.at[step, k],
                recv_sem=halo_recv.at[step, k ^ 1],
                device_id=neighbours[k],
                device_id_type=MESH,
            )
            copy.start()
            sends.append(copy)

    lane40 = lax.broadcasted_iota(jnp.int32, (40, LANES), 1)
    own_half = lane40 < 64

    def finish_halo(step, base):
        out = []
        for k in range(6):
            pltpu.make_async_copy(inbox.at[step, k], inbox.at[step, k], halo_recv.at[step, k]).wait()
            mine, got = part[step, k], pltpu.roll(inbox[step, k], 64, 1)
            total = jnp.where(exists[k], mine + got, jnp.where(own_half, mine, 0.0))
            if base is not None:
                total = base[k] + total
            out.append(total)
        last = part[step, 6]
        out.append(last if base is None else base[6] + last)
        return out

    def start_sum(buf, send_sem, recv_sem, which, slot, others, value):
        buf[which, pl.ds(slot, 1)] = value[None]
        for other in others:
            pltpu.make_async_remote_copy(
                src_ref=buf.at[which, pl.ds(slot, 1)],
                dst_ref=buf.at[which, pl.ds(slot, 1)],
                send_sem=send_sem.at[which],
                recv_sem=recv_sem.at[which],
                device_id=other,
                device_id_type=MESH,
            ).start()

    def wait_all(buf, sem, which, count):
        some = buf.at[which, pl.ds(0, count)]
        pltpu.make_async_copy(some, some, sem.at[which]).wait()

    def start_plane(which, value):
        start_sum(plane_buf, plane_send, plane_recv, which, plane_at, plane_devices, value)

    def plane_to_line(which):
        wait_all(plane_buf, plane_recv, which, PLANE - 1)
        value = jnp.sum(plane_buf[which].reshape(PLANE, LANES), axis=0, keepdims=True)
        start_sum(line_buf, line_send, line_recv, which, at["gz"], line_devices, value)

    def finish_line(which):
        wait_all(line_buf, line_recv, which, N_GZ - 1)
        return jnp.sum(line_buf[which].reshape(N_GZ, LANES), axis=0, keepdims=True)

    position = lax.broadcasted_iota(jnp.int32, (1, 384), 1)
    target = ((position // 64) * 128 + position % 64 + 1).astype(F32)
    face_col = lax.broadcasted_iota(jnp.int32, (512, 1), 0)
    sent = jnp.concatenate([send_ref[0:1, :], send_ref[1:2, :], send_ref[2:3, :]], axis=1)
    found = jnp.sum(jnp.where(face_col == sent, target, 0.0), axis=1, keepdims=True)
    inner = jnp.broadcast_to(jnp.where(found > 0.0, 0.0, 1.0), (512, LANES)).astype(BF16)
    below = jnp.where(
        lax.broadcasted_iota(jnp.int32, (512, 512), 1) < lax.broadcasted_iota(jnp.int32, (512, 512), 0), 1.0, 0.0
    ).astype(BF16)
    rank = dot(below, inner)
    new_place = jnp.where(jnp.broadcast_to(found, (512, LANES)) > 0.0, found - 1.0, 768.0 + rank)
    new_int = new_place.astype(jnp.int32)
    lane512 = lax.broadcasted_iota(jnp.int32, (512, LANES), 1)
    for t in range(7):
        place[:, LANES * t : LANES * (t + 1)] = onehot(new_int, lane512 + LANES * t)

    rhs = rhs_ref[...]
    placed = dot(jnp.concatenate(pieces(rhs, 3), axis=0).astype(BF16), place[...])
    placed = placed[0:40] + placed[40:80] + placed[80:120]
    for t in range(7):
        part[0, t] = placed[:, LANES * t : LANES * (t + 1)]
    pl.semaphore_wait(barrier, len(plane_devices) + len(line_devices))
    send_halo(0)

    place_row = new_place.T[0:8, :]
    high = jnp.floor(place_row * (1.0 / 32.0))
    digits = jnp.concatenate([high, place_row - 32.0 * high], axis=0).astype(BF16)
    row512 = lax.broadcasted_iota(jnp.int32, (512, 256), 0)
    row128 = lax.broadcasted_iota(jnp.int32, (LANES, 256), 0)
    for f in range(4):
        old = faces_ref[f : f + 1, :]
        looked = dot(digits, onehot(row512, old))
        owned = (looked[0:1] * 32.0 + looked[8:9]).astype(jnp.int32)
        slot = old - 512
        new = jnp.where(old < 512, owned, (slot // 64) * 128 + 64 + slot % 64)
        for t in range(7):
            pick[LANES * t : LANES * (t + 1), 256 * f : 256 * (f + 1)] = onehot(row128 + LANES * t, new)

    for k in range(8):
        piece = blocks_ref[:, 80 * k : 80 * k + 80]
        rows[pl.ds(k, 120, stride=8), :] = jnp.concatenate([piece, jnp.zeros((120, 48), F32)], axis=1)
    for b in range(6):
        both = jnp.concatenate(pieces(rows[160 * b : 160 * b + 160, :], 2), axis=1).astype(BF16)
        spread = dot(both, embed_ref[...])
        real, imag = spread[0:80], spread[80:160]
        block = jnp.concatenate([real[:, :512] - imag[:, 512:], imag[:, :512] + real[:, 512:]], axis=0)
        raw[160 * b : 160 * b + 160, :] = block
        smat[160 * b : 160 * b + 160, :] = block.astype(BF16)
    raw[960:1024, :] = jnp.zeros((64, 512), F32)
    smat_t[0:160, :] = raw[:, 0:256].T[0:160].astype(BF16)
    smat_t[160:320, :] = raw[:, 256:512].T[64:224].astype(BF16)
    zhi[960:1024, :] = jnp.zeros((64, 256), BF16)
    zlo[960:1024, :] = jnp.zeros((64, 256), BF16)
    weights = []
    for c in range(2):
        for d in range(3):
            factor = jnp.where(flag_ref[...] > 0, stretch_ref[d : d + 1, :], 1.0)
            weights.append(jnp.where(class_ref[...] == c, scale_ref[...] * factor, 0.0))

    def first_half(tiles):
        split = pieces(jnp.concatenate(tiles, axis=1), 2)
        picked = dot(jnp.concatenate(split, axis=0).astype(BF16), pick[...])
        upper = [picked[0:40, 256 * f : 256 * f + 256] for f in range(4)]
        lower = [picked[40:80, 256 * f : 256 * f + 256] for f in range(4)]
        stacked = jnp.concatenate(upper + lower + upper + [jnp.zeros((32, 256), F32)], axis=0).astype(BF16)
        energy = jnp.zeros((8, 256), F32)
        for b in range(6):
            projected = dot(smat[160 * b : 160 * b + 160, :], stacked)
            weighted = projected * weights[b]
            energy = energy + jnp.sum((weighted * projected).reshape(20, 8, 256), axis=0)
            head, tail = pieces(weighted, 2)
            zhi[160 * b : 160 * b + 160, :] = head.astype(BF16)
            zlo[160 * b : 160 * b + 160, :] = tail.astype(BF16)
        return energy

    def second_half(step):
        both = dot(smat_t[...], zhi[...])
        image = both[0:160] + both[160:320] + dot(smat_t[0:160, :], zlo[...])
        wide = jnp.concatenate([image[40 * f : 40 * f + 40] for f in range(4)], axis=1)
        spread = dot_nt(jnp.concatenate(pieces(wide, 3), axis=0).astype(BF16), pick[...])
        spread = spread[0:40] + spread[40:80] + spread[80:120]
        for t in range(7):
            part[step, t] = spread[:, LANES * t : LANES * (t + 1)]
        send_halo(step)

    def own(tiles):
        return [jnp.where(own_half, x, 0.0) for x in tiles[:6]] + [tiles[6]]

    def product(mine, tiles):
        total = mine[0] * tiles[0]
        for t in range(1, 7):
            total = total + mine[t] * tiles[t]
        return jnp.sum(total, axis=0, keepdims=True)

    def energy_row(energy):
        row = jnp.sum(energy, axis=0, keepdims=True)
        return row[:, 0:128] + row[:, 128:256]

    def to_lanes(lines):
        square = jnp.concatenate(lines + [jnp.zeros((16 - len(lines), LANES), F32)], axis=0)
        sums = jnp.sum(square, axis=1, keepdims=True)
        on_diagonal = lax.broadcasted_iota(jnp.int32, (16, LANES), 0) == lax.broadcasted_iota(jnp.int32, (16, LANES), 1)
        return jnp.sum(jnp.where(on_diagonal, sums, 0.0), axis=0, keepdims=True)

    def scalar(line, q):
        return jnp.broadcast_to(line[:, q : q + 1], (1, LANES))

    def combine(terms):
        total = None
        for factor, value in terms:
            total = factor * value if total is None else total + factor * value
        return total

    def lincomb(*terms):
        return [combine([(factor, tiles[t]) for factor, tiles in terms]) for t in range(7)]

    def back(tiles_list):
        stack = []
        for tiles in tiles_list:
            stack += pieces(jnp.concatenate(tiles, axis=1), 3)
        moved = dot_nt(jnp.concatenate(stack, axis=0).astype(BF16), place[...])
        out = []
        for i in range(len(tiles_list)):
            out.append(moved[120 * i : 120 * i + 40] + moved[120 * i + 40 : 120 * i + 80] + moved[120 * i + 80 : 120 * i + 120])
        return out

    first = finish_halo(0, None)
    energy = first_half(first)
    norm_row = product(own(first), first)
    start_plane(0, to_lanes([norm_row, norm_row + energy_row(energy)]))
    second_half(1)
    plane_to_line(0)
    image1 = finish_halo(1, first)
    first_half(image1)
    second_half(2)
    totals = finish_line(0)
    image2 = finish_halo(2, image1)

    norm0, curve0 = scalar(totals, 0), scalar(totals, 1)
    alpha0 = norm0 / curve0
    rho = SHIFT * curve0 / norm0
    eta = 1.0 / jnp.sqrt(norm0)
    inv_eta = 1.0 / eta
    inv_theta = 1.0 / THETA

    unit = lincomb((eta, first))
    res1 = lincomb((eta, first), (-eta * alpha0, image1))
    krylov1 = lincomb((eta * inv_theta, image1), (-eta * alpha0 * inv_theta, image2), (-rho * inv_theta, res1))
    first_half(krylov1)
    second_half(3)
    image3 = finish_halo(3, krylov1)
    krylov2 = lincomb((inv_theta, image3), (-rho * inv_theta, krylov1))

    energy = first_half(krylov2)
    basis = [unit, res1, krylov1, krylov2]
    masked = [own(tiles) for tiles in basis]
    pairs = [(0, 1), (0, 2), (0, 3), (1, 1), (1, 2), (1, 3), (2, 2), (2, 3), (3, 3)]
    lines = [product(masked[i], basis[j]) for i, j in pairs]
    start_plane(1, to_lanes(lines + [lines[-1] + energy_row(energy)]))
    second_half(4)
    plane_to_line(1)
    res1_own, krylov1_own, krylov2_own = back([res1, krylov1, krylov2])
    image4 = finish_halo(4, krylov2)
    krylov3_own = back([lincomb((inv_theta, image4), (-rho * inv_theta, krylov2))])[0]
    totals = finish_line(1)

    gram = {(0, 0): eta * eta * norm0}
    for q, (i, j) in enumerate(pairs):
        gram[i, j] = gram[j, i] = scalar(totals, q)
    inv_alpha0 = 1.0 / alpha0
    gram[3, 4] = (scalar(totals, 9) - rho * gram[3, 3]) * inv_theta
    gram[2, 4] = gram[3, 3]
    gram[1, 4] = gram[2, 3]
    gram[0, 4] = ((gram[0, 3] - gram[1, 3]) * inv_alpha0 - rho * gram[0, 3]) * inv_theta

    def apply(p):
        scaled = p[0] * inv_alpha0
        out = [scaled, rho * p[1] - scaled]
        for i in range(2, len(p)):
            out.append(rho * p[i] + THETA * p[i - 1])
        return out + [THETA * p[-1]]

    def form(a, b):
        return combine([(x, combine([(y, gram[i, j]) for j, y in enumerate(b)])) for i, x in enumerate(a)])

    norm = gram[1, 1]
    zero = jnp.zeros((1, LANES), F32)
    sol = [alpha0, zero, zero, zero]
    res = [zero, zero + 1.0]
    direction = [norm / gram[0, 0], zero + 1.0]
    for i in range(3):
        image = apply(direction)
        alpha = norm / form(direction, image)
        for j, x in enumerate(direction):
            sol[j] = sol[j] + alpha * x
        res = res + [zero]
        res = [x - alpha * y for x, y in zip(res, image)]
        if i < 2:
            new = form(res, res)
            beta = new / norm
            direction = [x + beta * y for x, y in zip(res, direction + [zero])]
            norm = new

    def wide(line):
        return jnp.concatenate([line] * 4, axis=1)

    sol_ref[...] = combine(
        [
            (wide(sol[0]), rhs),
            (wide(sol[1] * inv_eta), res1_own),
            (wide(sol[2] * inv_eta), krylov1_own),
            (wide(sol[3] * inv_eta), krylov2_own),
        ]
    )
    res_ref[...] = combine(
        [
            (wide(res[0]), rhs),
            (wide(res[1] * inv_eta), res1_own),
            (wide(res[2] * inv_eta), krylov1_own),
            (wide(res[3] * inv_eta), krylov2_own),
            (wide(res[4] * inv_eta), krylov3_own),
        ]
    )
    for copy in sends:
        copy.wait_send()
    for which in range(2):
        wait_all(plane_buf, plane_send, which, PLANE - 1)
        wait_all(line_buf, line_send, which, N_GZ - 1)


def local(right_side, elem_faces, elem_class, elem_scale, stretch, pml_flag, send_faces, blocks):
    vmem = pl.BlockSpec(memory_space=pltpu.VMEM)
    steps = 5
    field = jax.ShapeDtypeStruct((40, 512), F32)
    solution_field, residual = pl.pallas_call(
        kernel,
        out_shape=(field, field),
        in_specs=[vmem] * 9,
        out_specs=(vmem, vmem),
        scratch_shapes=[
            pltpu.VMEM((512, 896), BF16),
            pltpu.VMEM((896, 1024), BF16),
            pltpu.VMEM((1024, 512), F32),
            pltpu.VMEM((960, 512), BF16),
            pltpu.VMEM((320, 1024), BF16),
            pltpu.VMEM((960, LANES), F32),
            pltpu.VMEM((1024, 256), BF16),
            pltpu.VMEM((1024, 256), BF16),
            pltpu.VMEM((steps, 7, 40, LANES), F32),
            pltpu.VMEM((steps, 6, 40, LANES), F32),
            pltpu.VMEM((2, PLANE, 1, LANES), F32),
            pltpu.VMEM((2, N_GZ, 1, LANES), F32),
            pltpu.SemaphoreType.DMA((steps, 6)),
            pltpu.SemaphoreType.DMA((steps, 6)),
            pltpu.SemaphoreType.DMA((2,)),
            pltpu.SemaphoreType.DMA((2,)),
            pltpu.SemaphoreType.DMA((2,)),
            pltpu.SemaphoreType.DMA((2,)),
        ],
        compiler_params=pltpu.CompilerParams(
            collective_id=0, has_side_effects=True, vmem_limit_bytes=40 * 1024 * 1024
        ),
    )(
        right_side.reshape(40, 512),
        elem_faces.reshape(4, 256),
        elem_class.reshape(1, 256),
        elem_scale.reshape(1, 256),
        stretch.reshape(3, 256),
        pml_flag.reshape(1, 256),
        send_faces.reshape(3, 128),
        blocks.reshape(120, 640),
        jnp.asarray(embed_matrix(), BF16),
    )
    return solution_field.reshape(right_side.shape), residual.reshape(right_side.shape)


def solution(mesh):
    in_specs = (
        P(None, "gx", "gy", "gz"),
        P(None, "gx", "gy", "gz"),
        P("gx", "gy", "gz"),
        P("gx", "gy", "gz"),
        P(None, "gx", "gy", "gz"),
        P("gx", "gy", "gz"),
        P(None, "gx", "gy", "gz"),
        P(),
    )
    out_specs = (P(None, "gx", "gy", "gz"), P(None, "gx", "gy", "gz"))
    return jax.shard_map(local, mesh=mesh, in_specs=in_specs, out_specs=out_specs, check_vma=False)
```

```python
import functools

import jax
import jax.numpy as jnp
import numpy as np
from jax import lax
from jax.experimental import pallas as pl
from jax.experimental.pallas import tpu as pltpu
from jax.sharding import PartitionSpec as P

MESH = pl.DeviceIdType.MESH
F32 = jnp.float32
BF16 = jnp.bfloat16
N_GX, N_GY, N_GZ = 8, 4, 16
AXES = (("gx", N_GX), ("gy", N_GY), ("gz", N_GZ))
PLANE = N_GX * N_GY
LANES = 128
EARLY = 640
TILE = (0, 1, 2, 3, 5, 6)
STEPS = 5


def dot(a, b):
    return jnp.dot(a, b, preferred_element_type=F32)


def dot_nt(a, b):
    return lax.dot_general(a, b, (((1,), (1,)), ((), ())), preferred_element_type=F32)


def pieces(value, count):
    out = []
    for _ in range(count):
        head = value.astype(BF16).astype(F32)
        out.append(head)
        value = value - head
    return out


def onehot(left, right):
    return jnp.where(left == right, 1.0, 0.0).astype(BF16)


def embed_rows():
    column = lax.broadcasted_iota(jnp.int32, (1, 1024), 1)
    part, inside = column // 512, column % 512
    copy, place = inside // 160, inside % 160
    face, rest = place // 40, place % 40
    row = face * 20 + rest % 20 + jnp.where(copy == 2, 128, 0)
    return jnp.where((copy < 3) & (rest // 20 == part), row, -1)


def kernel(
    rhs_in,
    faces_in,
    class_in,
    scale_in,
    stretch_in,
    flag_in,
    send_in,
    blocks_in,
    sol_ref,
    res_ref,
    rhs_ref,
    faces_ref,
    class_ref,
    scale_ref,
    stretch_ref,
    flag_ref,
    send_ref,
    blocks_ref,
    lines640,
    embed,
    place,
    pick,
    raw,
    smat,
    smat_t,
    rows,
    zhi,
    zlo,
    part,
    inbox,
    plane_buf,
    line_buf,
    halo_send,
    halo_recv,
    plane_send,
    plane_recv,
    line_send,
    line_recv,
    load_sem,
):
    at = {name: lax.axis_index(name) for name, _ in AXES}
    size = dict(AXES)

    def device(**moved):
        return tuple(moved.get(name, at[name]) for name, _ in AXES)

    neighbours, exists = [], []
    for name, n in AXES:
        neighbours.append(device(**{name: lax.rem(at[name] + (n - 1), n)}))
        neighbours.append(device(**{name: lax.rem(at[name] + 1, n)}))
        exists.append(at[name] > 0)
        exists.append(at[name] < n - 1)
    plane_at = at["gx"] * N_GY + at["gy"]
    offsets = [(dx, dy) for dx in range(N_GX) for dy in range(N_GY) if dx or dy]
    offsets.sort(key=lambda d: -(min(d[0], N_GX - d[0]) // 2 + min(d[1], N_GY - d[1])))
    plane_devices = []
    for dx, dy in offsets:
        plane_devices.append(device(gx=lax.rem(at["gx"] + dx, N_GX), gy=lax.rem(at["gy"] + dy, N_GY)))
    line_devices = []
    for step in sorted(range(1, N_GZ), key=lambda d: -min(d, N_GZ - d)):
        line_devices.append(device(gz=lax.rem(at["gz"] + step, N_GZ)))

    barrier = pltpu.get_barrier_semaphore()
    for other in plane_devices + line_devices:
        pl.semaphore_signal(barrier, inc=1, device_id=other, device_id_type=MESH)

    loads = []
    held = (send_ref, rhs_ref, faces_ref, blocks_ref, class_ref, scale_ref, stretch_ref, flag_ref)
    given = (send_in, rhs_in, faces_in, blocks_in, class_in, scale_in, stretch_in, flag_in)
    for i, (there, here) in enumerate(zip(given, held)):
        copy = pltpu.make_async_copy(there, here, load_sem.at[i])
        copy.start()
        loads.append(copy)

    sends = []

    def send_halo(step, directions):
        for k in directions:
            copy = pltpu.make_async_remote_copy(
                src_ref=part.at[step, TILE[k]],
                dst_ref=inbox.at[step, k ^ 1],
                send_sem=halo_send.at[step, k],
                recv_sem=halo_recv.at[step, k ^ 1],
                device_id=neighbours[k],
                device_id_type=MESH,
            )
            copy.start()
            sends.append(copy)

    lane40 = lax.broadcasted_iota(jnp.int32, (40, LANES), 1)
    own_half = lane40 < 64

    def receive(step, k):
        pltpu.make_async_copy(inbox.at[step, k], inbox.at[step, k], halo_recv.at[step, k]).wait()
        mine, got = part[step, TILE[k]], pltpu.roll(inbox[step, k], 64, 1)
        return jnp.where(exists[k], mine + got, jnp.where(own_half, mine, 0.0))

    def start_sum(buf, send_sem, recv_sem, which, slot, others, value):
        buf[which, pl.ds(slot, 1)] = value[None]
        for other in others:
            pltpu.make_async_remote_copy(
                src_ref=buf.at[which, pl.ds(slot, 1)],
                dst_ref=buf.at[which, pl.ds(slot, 1)],
                send_sem=send_sem.at[which],
                recv_sem=recv_sem.at[which],
                device_id=other,
                device_id_type=MESH,
            ).start()

    def wait_all(buf, sem, which, count):
        some = buf.at[which, pl.ds(0, count)]
        pltpu.make_async_copy(some, some, sem.at[which]).wait()

    def start_plane(which, value):
        start_sum(plane_buf, plane_send, plane_recv, which, plane_at, plane_devices, value)

    def plane_to_line(which):
        wait_all(plane_buf, plane_recv, which, PLANE - 1)
        value = jnp.sum(plane_buf[which], axis=0)
        start_sum(line_buf, line_send, line_recv, which, at["gz"], line_devices, value)

    def finish_line(which):
        wait_all(line_buf, line_recv, which, N_GZ - 1)
        return jnp.sum(line_buf[which], axis=0)

    position = lax.broadcasted_iota(jnp.int32, (1, 384), 1)
    target = ((position // 64) * 128 + jnp.where(position >= 256, 128, 0) + position % 64 + 1).astype(F32)
    face_col = lax.broadcasted_iota(jnp.int32, (512, 1), 0)
    loads[0].wait()
    sent = jnp.concatenate([send_ref[k, 0] for k in range(6)], axis=1)
    found = jnp.sum(jnp.where(face_col == sent, target, 0.0), axis=1, keepdims=True)
    inner = jnp.broadcast_to(jnp.where(found > 0.0, 0.0, 1.0), (512, LANES)).astype(BF16)
    below = jnp.where(
        lax.broadcasted_iota(jnp.int32, (512, 512), 1) < lax.broadcasted_iota(jnp.int32, (512, 512), 0), 1.0, 0.0
    ).astype(BF16)
    rank = dot(below, inner)
    new_place = jnp.where(jnp.broadcast_to(found, (512, LANES)) > 0.0, found - 1.0, 512.0 + rank)
    new_int = new_place.astype(jnp.int32)
    lane512 = lax.broadcasted_iota(jnp.int32, (512, LANES), 1)
    for t in range(7):
        place[:, LANES * t : LANES * (t + 1)] = onehot(new_int, lane512 + LANES * t)

    loads[1].wait()
    rhs = rhs_ref[:, 0, 0, :]
    placed = dot(jnp.concatenate(pieces(rhs, 3), axis=0).astype(BF16), place[...])
    placed = placed[0:40] + placed[40:80] + placed[80:120]
    for t in range(7):
        part[0, t] = placed[:, LANES * t : LANES * (t + 1)]
    pl.semaphore_wait(barrier, len(plane_devices) + len(line_devices))
    send_halo(0, (4, 5, 2, 3, 0, 1))

    place_row = new_place.T[0:8, :]
    high = jnp.floor(place_row * (1.0 / 32.0))
    digits = jnp.concatenate([high, place_row - 32.0 * high], axis=0).astype(BF16)
    row512 = lax.broadcasted_iota(jnp.int32, (512, 256), 0)
    row128 = lax.broadcasted_iota(jnp.int32, (LANES, 256), 0)
    loads[2].wait()
    for f in range(4):
        old = faces_ref[f, 0]
        looked = dot(digits, onehot(row512, old))
        owned = (looked[0:1] * 32.0 + looked[8:9]).astype(jnp.int32)
        slot = old - 512
        new = jnp.where(old < 512, owned, (slot // 64) * 128 + jnp.where(slot >= 256, 128, 0) + 64 + slot % 64)
        for t in range(7):
            pick[LANES * t : LANES * (t + 1), 256 * f : 256 * (f + 1)] = onehot(row128 + LANES * t, new)

    embed[...] = onehot(lax.broadcasted_iota(jnp.int32, (256, 1024), 0), embed_rows())
    loads[3].wait()
    for b in range(6):
        for g in range(10):
            lines640[20 * b + 2 * g : 20 * b + 2 * g + 2, :] = blocks_ref[b // 3, b % 3, :, 640 * g : 640 * g + 640]
    for k in range(8):
        piece = lines640[:, 80 * k : 80 * k + 80]
        rows[pl.ds(k, 120, stride=8), :] = jnp.concatenate([piece, jnp.zeros((120, 48), F32)], axis=1)
    for b in range(6):
        both = jnp.concatenate(pieces(rows[160 * b : 160 * b + 160, :], 2), axis=1).astype(BF16)
        spread = dot(both, embed[...]).reshape(10, 2, 8, 1024)
        real, imag = spread[:, 0].reshape(80, 1024), spread[:, 1].reshape(80, 1024)
        block = jnp.concatenate([real[:, :512] - imag[:, 512:], imag[:, :512] + real[:, 512:]], axis=0)
        raw[160 * b : 160 * b + 160, :] = block
        smat[160 * b : 160 * b + 160, :] = block.astype(BF16)
    raw[960:1024, :] = jnp.zeros((64, 512), F32)
    smat_t[0:160, :] = raw[:, 0:256].T[0:160].astype(BF16)
    smat_t[160:320, :] = raw[:, 256:512].T[64:224].astype(BF16)
    zhi[960:1024, :] = jnp.zeros((64, 256), BF16)
    zlo[960:1024, :] = jnp.zeros((64, 256), BF16)
    for copy in loads[4:]:
        copy.wait()
    weights = []
    for c in range(2):
        for d in range(3):
            factor = jnp.where(flag_ref[0] > 0, stretch_ref[d, 0], 1.0)
            weights.append(jnp.where(class_ref[0] == c, scale_ref[0] * factor, 0.0))

    def gather(tiles, low, high):
        split = pieces(jnp.concatenate(tiles, axis=1), 2)
        return dot(jnp.concatenate(split, axis=0).astype(BF16), pick[low:high, :])

    def project(picked, with_energy):
        upper = [picked[0:40, 256 * f : 256 * f + 256] for f in range(4)]
        lower = [picked[40:80, 256 * f : 256 * f + 256] for f in range(4)]
        stacked = jnp.concatenate(upper + lower + upper + [jnp.zeros((32, 256), F32)], axis=0).astype(BF16)
        energy = jnp.zeros((8, 256), F32)
        for b in range(6):
            projected = dot(smat[160 * b : 160 * b + 160, :], stacked)
            weighted = projected * weights[b]
            if with_energy:
                energy = energy + jnp.sum((weighted * projected).reshape(20, 8, 256), axis=0)
            head, tail = pieces(weighted, 2)
            zhi[160 * b : 160 * b + 160, :] = head.astype(BF16)
            zlo[160 * b : 160 * b + 160, :] = tail.astype(BF16)
        return energy

    def scatter(step):
        both = dot(smat_t[...], zhi[...])
        image = both[0:160] + both[160:320] + dot(smat_t[0:160, :], zlo[...])
        wide = jnp.concatenate([image[40 * f : 40 * f + 40] for f in range(4)], axis=1)
        split = jnp.concatenate(pieces(wide, 3), axis=0).astype(BF16)
        for tiles, directions in (((5, 6), (4, 5)), ((2, 3), (2, 3)), ((0, 1), (0, 1)), ((4,), ())):
            low = LANES * tiles[0]
            spread = dot_nt(split, pick[low : low + LANES * len(tiles), :])
            spread = spread[0:40] + spread[40:80] + spread[80:120]
            for n, t in enumerate(tiles):
                part[step, t] = spread[:, LANES * n : LANES * (n + 1)]
            send_halo(step, directions)

    def own(tiles):
        return [x if t == 4 else jnp.where(own_half, x, 0.0) for t, x in enumerate(tiles)]

    def product(mine, tiles):
        total = mine[0] * tiles[0]
        for t in range(1, 7):
            total = total + mine[t] * tiles[t]
        return jnp.sum(total, axis=0, keepdims=True)

    def energy_row(energy):
        row = jnp.sum(energy, axis=0, keepdims=True)
        return row[:, 0:128] + row[:, 128:256]

    def to_lanes(lines):
        square = jnp.concatenate(lines + [jnp.zeros((16 - len(lines), LANES), F32)], axis=0)
        sums = jnp.sum(square, axis=1, keepdims=True)
        on_diagonal = lax.broadcasted_iota(jnp.int32, (16, LANES), 0) == lax.broadcasted_iota(jnp.int32, (16, LANES), 1)
        return jnp.sum(jnp.where(on_diagonal, sums, 0.0), axis=0, keepdims=True)

    def scalar(line, q):
        return jnp.broadcast_to(line[:, q : q + 1], (1, LANES))

    def combine(terms):
        total = None
        for factor, value in terms:
            total = factor * value if total is None else total + factor * value
        return total

    def back(tiles_list):
        stack = []
        for tiles in tiles_list:
            stack += pieces(jnp.concatenate(tiles, axis=1), 3)
        moved = dot_nt(jnp.concatenate(stack, axis=0).astype(BF16), place[...])
        out = []
        for i in range(len(tiles_list)):
            out.append(moved[120 * i : 120 * i + 40] + moved[120 * i + 40 : 120 * i + 80] + moved[120 * i + 80 : 120 * i + 120])
        return out

    total = blocks_ref[...]
    total = jnp.sum(total * total, axis=(0, 1, 2))
    rho = 1.0 + jnp.sum(total.reshape(1, 6400), axis=1, keepdims=True) * (3.0 / 160.0)
    rho = jnp.broadcast_to(rho, (1, LANES))
    theta = 256.0 * rho
    inv_theta = 1.0 / theta
    keep = (1.0 - rho) * inv_theta

    basis, masked, sums, moved = [], [], {}, [rhs]

    def advance(step):
        def tile(t, got):
            return got if step == 0 else keep * basis[-1][t] + inv_theta * got

        early = [tile(k, receive(step, k)) for k in range(4)] + [tile(4, part[step, 4])]
        picked = gather(early, 0, EARLY) if step < 4 else None
        late = [tile(TILE[k], receive(step, k)) for k in (4, 5)]
        if step < 4:
            picked = picked + gather(late, EARLY, 896)
        basis.append(early + late)
        return picked

    def inner(i, j):
        sums[i, j] = product(masked[i], basis[j])

    for step in range(3):
        project(advance(step), False)
        masked.append(own(basis[step]))
        scatter(step + 1)
        for i in range(step + 1):
            inner(i, step)
        if step:
            moved += back([basis[step]])
    energy = project(advance(3), True)
    masked.append(own(basis[3]))
    for i in range(4):
        inner(i, 3)
    pairs = [(i, j) for i in range(4) for j in range(i, 4)]
    start_plane(0, to_lanes([sums[pair] for pair in pairs] + [sums[3, 3] + energy_row(energy)]))
    scatter(4)
    plane_to_line(0)
    moved += back([basis[3]])
    advance(4)
    moved += back([basis[4]])
    totals = finish_line(0)

    gram = {}
    for q, (i, j) in enumerate(pairs):
        gram[i, j] = gram[j, i] = scalar(totals, q)
    gram[3, 4] = (scalar(totals, len(pairs)) - rho * gram[3, 3]) * inv_theta
    gram[2, 4] = gram[3, 3]
    gram[1, 4] = gram[2, 3]
    gram[0, 4] = gram[1, 3]

    def apply(p):
        out = [rho * p[0]]
        for i in range(1, len(p)):
            out.append(rho * p[i] + theta * p[i - 1])
        return out + [theta * p[-1]]

    def form(a, b):
        return combine([(x, combine([(y, gram[i, j]) for j, y in enumerate(b)])) for i, x in enumerate(a)])

    norm = gram[0, 0]
    zero = jnp.zeros((1, LANES), F32)
    sol, res, direction = [zero] * 4, [zero + 1.0], [zero + 1.0]
    for i in range(4):
        image = apply(direction)
        alpha = norm / form(direction, image)
        for j, x in enumerate(direction):
            sol[j] = sol[j] + alpha * x
        res = [x - alpha * y for x, y in zip(res + [zero], image)]
        if i < 3:
            new = form(res, res)
            beta = new / norm
            direction = [x + beta * y for x, y in zip(res, direction + [zero])]
            norm = new

    def wide(line):
        return jnp.concatenate([line] * 4, axis=1)

    sol_ref[:, 0, 0, :] = combine([(wide(c), x) for c, x in zip(sol, moved)])
    res_ref[:, 0, 0, :] = combine([(wide(c), x) for c, x in zip(res, moved)])
    for copy in sends:
        copy.wait_send()
    wait_all(plane_buf, plane_send, 0, PLANE - 1)
    wait_all(line_buf, line_send, 0, N_GZ - 1)


def local(right_side, elem_faces, elem_class, elem_scale, stretch, pml_flag, send_faces, blocks):
    vmem = pl.BlockSpec(memory_space=pltpu.VMEM)
    field = jax.ShapeDtypeStruct(right_side.shape, F32)
    given = (right_side, elem_faces, elem_class, elem_scale, stretch, pml_flag, send_faces, blocks)
    solution_field, residual = pl.pallas_call(
        kernel,
        out_shape=(field, field),
        in_specs=[pl.BlockSpec(memory_space=pltpu.HBM)] * len(given),
        out_specs=(vmem, vmem),
        scratch_shapes=[pltpu.VMEM(x.shape, x.dtype) for x in given]
        + [
            pltpu.VMEM((120, 640), F32),
            pltpu.VMEM((256, 1024), BF16),
            pltpu.VMEM((512, 896), BF16),
            pltpu.VMEM((896, 1024), BF16),
            pltpu.VMEM((1024, 512), F32),
            pltpu.VMEM((960, 512), BF16),
            pltpu.VMEM((320, 1024), BF16),
            pltpu.VMEM((960, LANES), F32),
            pltpu.VMEM((1024, 256), BF16),
            pltpu.VMEM((1024, 256), BF16),
            pltpu.VMEM((STEPS, 7, 40, LANES), F32),
            pltpu.VMEM((STEPS, 6, 40, LANES), F32),
            pltpu.VMEM((1, PLANE, 1, LANES), F32),
            pltpu.VMEM((1, N_GZ, 1, LANES), F32),
            pltpu.SemaphoreType.DMA((STEPS, 6)),
            pltpu.SemaphoreType.DMA((STEPS, 6)),
            pltpu.SemaphoreType.DMA((1,)),
            pltpu.SemaphoreType.DMA((1,)),
            pltpu.SemaphoreType.DMA((1,)),
            pltpu.SemaphoreType.DMA((1,)),
            pltpu.SemaphoreType.DMA((len(given),)),
        ],
        compiler_params=pltpu.CompilerParams(
            collective_id=0, has_side_effects=True, vmem_limit_bytes=56 * 1024 * 1024
        ),
    )(*given)
    return solution_field, residual


def solution(mesh):
    in_specs = (
        P(None, "gx", "gy", "gz"),
        P(None, "gx", "gy", "gz"),
        P("gx", "gy", "gz"),
        P("gx", "gy", "gz"),
        P(None, "gx", "gy", "gz"),
        P("gx", "gy", "gz"),
        P(None, "gx", "gy", "gz"),
        P(),
    )
    out_specs = (P(None, "gx", "gy", "gz"), P(None, "gx", "gy", "gz"))
    return jax.shard_map(local, mesh=mesh, in_specs=in_specs, out_specs=out_specs, check_vma=False)
```

```python
import functools

import jax
import jax.numpy as jnp
import numpy as np
from jax import lax
from jax.experimental import pallas as pl
from jax.experimental.pallas import tpu as pltpu
from jax.sharding import PartitionSpec as P

MESH = pl.DeviceIdType.MESH
F32 = jnp.float32
BF16 = jnp.bfloat16
N_GX, N_GY, N_GZ = 8, 4, 16
AXES = (("gx", N_GX), ("gy", N_GY), ("gz", N_GZ))
PLANE = N_GX * N_GY
LANES = 128
EARLY = 640
TILE = (0, 1, 2, 3, 5, 6)
STEPS = 5


def dot(a, b):
    return jnp.dot(a, b, preferred_element_type=F32)


def dot_nt(a, b):
    return lax.dot_general(a, b, (((1,), (1,)), ((), ())), preferred_element_type=F32)


def pieces(value, count):
    out = []
    for _ in range(count):
        head = value.astype(BF16).astype(F32)
        out.append(head)
        value = value - head
    return out


def onehot(left, right):
    return jnp.where(left == right, 1.0, 0.0).astype(BF16)


def embed_rows():
    column = lax.broadcasted_iota(jnp.int32, (1, 1024), 1)
    part, inside = column // 512, column % 512
    copy, place = inside // 160, inside % 160
    face, rest = place // 40, place % 40
    row = face * 20 + rest % 20 + jnp.where(copy == 2, 128, 0)
    return jnp.where((copy < 3) & (rest // 20 == part), row, -1)


def kernel(
    rhs_in,
    faces_in,
    class_in,
    scale_in,
    stretch_in,
    flag_in,
    send_in,
    blocks_in,
    out_ref,
    rhs_ref,
    faces_ref,
    class_ref,
    scale_ref,
    stretch_ref,
    flag_ref,
    send_ref,
    blocks_ref,
    lines640,
    embed,
    place,
    pick,
    pick_t,
    raw,
    smat,
    smat_t,
    rows,
    zhi,
    zlo,
    part,
    inbox,
    plane_buf,
    line_buf,
    halo_send,
    halo_recv,
    plane_send,
    plane_recv,
    line_send,
    line_recv,
    load_sem,
    near_sem,
    far_sem,
):
    at = {name: lax.axis_index(name) for name, _ in AXES}
    size = dict(AXES)

    def device(**moved):
        return tuple(moved.get(name, at[name]) for name, _ in AXES)

    neighbours, exists = [], []
    for name, n in AXES:
        neighbours.append(device(**{name: lax.rem(at[name] + (n - 1), n)}))
        neighbours.append(device(**{name: lax.rem(at[name] + 1, n)}))
        exists.append(at[name] > 0)
        exists.append(at[name] < n - 1)
    plane_at = at["gx"] * N_GY + at["gy"]
    offsets = [(dx, dy) for dx in range(N_GX) for dy in range(N_GY) if dx or dy]
    offsets.sort(key=lambda d: -(min(d[0], N_GX - d[0]) // 2 + min(d[1], N_GY - d[1])))
    plane_devices = []
    for dx, dy in offsets:
        plane_devices.append(device(gx=lax.rem(at["gx"] + dx, N_GX), gy=lax.rem(at["gy"] + dy, N_GY)))
    line_devices = []
    for step in sorted(range(1, N_GZ), key=lambda d: -min(d, N_GZ - d)):
        line_devices.append(device(gz=lax.rem(at["gz"] + step, N_GZ)))

    barrier = pltpu.get_barrier_semaphore()
    for other in neighbours:
        pl.semaphore_signal(barrier, inc=1, device_id=other, device_id_type=MESH)

    loads = []
    held = (send_ref, rhs_ref, faces_ref, blocks_ref, class_ref, scale_ref, stretch_ref, flag_ref)
    given = (send_in, rhs_in, faces_in, blocks_in, class_in, scale_in, stretch_in, flag_in)
    for i, (there, here) in enumerate(zip(given, held)):
        copy = pltpu.make_async_copy(there, here, load_sem.at[i])
        copy.start()
        loads.append(copy)

    def tell(sem, others):
        for other in others:
            pl.semaphore_signal(sem, inc=1, device_id=other, device_id_type=MESH)

    def along(name, *steps):
        return [device(**{name: lax.rem(at[name] + step, size[name])}) for step in steps]

    sends = []

    def send_halo(step, directions):
        for k in directions:
            copy = pltpu.make_async_remote_copy(
                src_ref=part.at[step, TILE[k]],
                dst_ref=inbox.at[step, k ^ 1],
                send_sem=halo_send.at[step, k],
                recv_sem=halo_recv.at[step, k ^ 1],
                device_id=neighbours[k],
                device_id_type=MESH,
            )
            copy.start()
            sends.append(copy)

    lane40 = lax.broadcasted_iota(jnp.int32, (40, LANES), 1)
    own_half = lane40 < 64

    def receive(step, k):
        pltpu.make_async_copy(inbox.at[step, k], inbox.at[step, k], halo_recv.at[step, k]).wait()
        mine, got = part[step, TILE[k]], pltpu.roll(inbox[step, k], 64, 1)
        return jnp.where(exists[k], mine + got, jnp.where(own_half, mine, 0.0))

    def start_sum(buf, send_sem, recv_sem, which, slot, others, value):
        buf[which, pl.ds(slot, 1)] = value[None]
        for other in others:
            pltpu.make_async_remote_copy(
                src_ref=buf.at[which, pl.ds(slot, 1)],
                dst_ref=buf.at[which, pl.ds(slot, 1)],
                send_sem=send_sem.at[which],
                recv_sem=recv_sem.at[which],
                device_id=other,
                device_id_type=MESH,
            ).start()

    def wait_all(buf, sem, which, count):
        some = buf.at[which, pl.ds(0, count)]
        pltpu.make_async_copy(some, some, sem.at[which]).wait()

    def start_plane(which, value):
        start_sum(plane_buf, plane_send, plane_recv, which, plane_at, plane_devices, value)

    def plane_to_line(which):
        wait_all(plane_buf, plane_recv, which, PLANE - 1)
        value = jnp.sum(plane_buf[which], axis=0)
        start_sum(line_buf, line_send, line_recv, which, at["gz"], line_devices, value)

    def finish_line(which):
        wait_all(line_buf, line_recv, which, N_GZ - 1)
        return jnp.sum(line_buf[which], axis=0)

    face512 = lax.broadcasted_iota(jnp.int32, (512, LANES), 0)
    no_face = jnp.full((1, 64), -1, jnp.int32)
    loads[0].wait()
    for k in range(6):
        shared = jnp.concatenate([send_ref[k, 0], no_face], axis=1)
        place[:, LANES * TILE[k] : LANES * (TILE[k] + 1)] = onehot(face512, shared)
    loads[1].wait()
    rhs = rhs_ref[:, 0, 0, :]
    rhs_split = jnp.concatenate(pieces(rhs, 3), axis=0).astype(BF16)

    def put(low, high):
        placed = dot(rhs_split, place[:, LANES * low : LANES * high])
        placed = placed[0:40] + placed[40:80] + placed[80:120]
        for t in range(low, high):
            part[0, t] = placed[:, LANES * (t - low) : LANES * (t - low + 1)]

    put(5, 7)
    put(0, 4)
    pl.semaphore_wait(barrier, 6)
    send_halo(0, (4, 5, 2, 3, 0, 1))

    position = lax.broadcasted_iota(jnp.int32, (1, 384), 1)
    target = ((position // 64) * 128 + jnp.where(position >= 256, 128, 0) + position % 64 + 1).astype(F32)
    face_col = lax.broadcasted_iota(jnp.int32, (512, 1), 0)
    sent = jnp.concatenate([send_ref[k, 0] for k in range(6)], axis=1)
    found = jnp.sum(jnp.where(face_col == sent, target, 0.0), axis=1, keepdims=True)
    inner = jnp.broadcast_to(jnp.where(found > 0.0, 0.0, 1.0), (512, LANES)).astype(BF16)
    below = jnp.where(
        lax.broadcasted_iota(jnp.int32, (512, 512), 1) < lax.broadcasted_iota(jnp.int32, (512, 512), 0), 1.0, 0.0
    ).astype(BF16)
    rank = dot(below, inner)
    new_place = jnp.where(jnp.broadcast_to(found, (512, LANES)) > 0.0, found - 1.0, 512.0 + rank)
    lane512 = lax.broadcasted_iota(jnp.int32, (512, LANES), 1)
    place[:, 512:640] = onehot(new_place.astype(jnp.int32), lane512 + 512)
    put(4, 5)

    place_row = new_place.T[0:8, :]
    high = jnp.floor(place_row * (1.0 / 32.0))
    digits = jnp.concatenate([high, place_row - 32.0 * high], axis=0).astype(BF16)
    row512 = lax.broadcasted_iota(jnp.int32, (512, 256), 0)
    row128 = lax.broadcasted_iota(jnp.int32, (LANES, 256), 0)
    lane256 = lax.broadcasted_iota(jnp.int32, (256, LANES), 1)
    loads[2].wait()
    for f in range(4):
        old = faces_ref[f, 0]
        looked = dot(digits, onehot(row512, old))
        owned = (looked[0:1] * 32.0 + looked[8:9]).astype(jnp.int32)
        slot = old - 512
        new = jnp.where(old < 512, owned, (slot // 64) * 128 + jnp.where(slot >= 256, 128, 0) + 64 + slot % 64)
        for t in range(7):
            pick[LANES * t : LANES * (t + 1), 256 * f : 256 * (f + 1)] = onehot(row128 + LANES * t, new)
        column = jnp.broadcast_to(new.astype(F32), (LANES, 256)).T.astype(jnp.int32)
        for t in range(7):
            pick_t[256 * f : 256 * (f + 1), LANES * t : LANES * (t + 1)] = onehot(column, lane256 + LANES * t)

    embed[...] = onehot(lax.broadcasted_iota(jnp.int32, (256, 1024), 0), embed_rows())
    loads[3].wait()
    for b in range(6):
        for g in range(10):
            lines640[20 * b + 2 * g : 20 * b + 2 * g + 2, :] = blocks_ref[b // 3, b % 3, :, 640 * g : 640 * g + 640]
    for k in range(8):
        piece = lines640[:, 80 * k : 80 * k + 80]
        rows[pl.ds(k, 120, stride=8), :] = jnp.concatenate([piece, jnp.zeros((120, 48), F32)], axis=1)
    for b in range(6):
        both = jnp.concatenate(pieces(rows[160 * b : 160 * b + 160, :], 2), axis=1).astype(BF16)
        spread = dot(both, embed[...]).reshape(10, 2, 8, 1024)
        real, imag = spread[:, 0].reshape(80, 1024), spread[:, 1].reshape(80, 1024)
        block = jnp.concatenate([real[:, :512] - imag[:, 512:], imag[:, :512] + real[:, 512:]], axis=0)
        raw[160 * b : 160 * b + 160, :] = block
        smat[160 * b : 160 * b + 160, :] = block.astype(BF16)
    raw[960:1024, :] = jnp.zeros((64, 512), F32)
    smat_t[0:160, :] = raw[:, 0:256].T[0:160].astype(BF16)
    smat_t[160:320, :] = raw[:, 256:512].T[64:224].astype(BF16)
    zhi[960:1024, :] = jnp.zeros((64, 256), BF16)
    zlo[960:1024, :] = jnp.zeros((64, 256), BF16)
    for copy in loads[4:]:
        copy.wait()
    weights = []
    for c in range(2):
        for d in range(3):
            factor = jnp.where(flag_ref[0] > 0, stretch_ref[d, 0], 1.0)
            weights.append(jnp.where(class_ref[0] == c, scale_ref[0] * factor, 0.0))

    def gather(tiles, low, high):
        split = pieces(jnp.concatenate(tiles, axis=1), 2)
        return dot(jnp.concatenate(split, axis=0).astype(BF16), pick[low:high, :])

    def project(picked, with_energy):
        upper = [picked[0:40, 256 * f : 256 * f + 256] for f in range(4)]
        lower = [picked[40:80, 256 * f : 256 * f + 256] for f in range(4)]
        stacked = jnp.concatenate(upper + lower + upper + [jnp.zeros((32, 256), F32)], axis=0).astype(BF16)
        energy = jnp.zeros((8, 256), F32)
        for b in range(6):
            projected = dot(smat[160 * b : 160 * b + 160, :], stacked)
            weighted = projected * weights[b]
            if with_energy:
                energy = energy + jnp.sum((weighted * projected).reshape(20, 8, 256), axis=0)
            head, tail = pieces(weighted, 2)
            zhi[160 * b : 160 * b + 160, :] = head.astype(BF16)
            zlo[160 * b : 160 * b + 160, :] = tail.astype(BF16)
        return energy

    def scatter(step):
        both = dot(smat_t[...], zhi[...])
        image = both[0:160] + both[160:320] + dot(smat_t[0:160, :], zlo[...])
        wide = jnp.concatenate([image[40 * f : 40 * f + 40] for f in range(4)], axis=1)
        split = jnp.concatenate(pieces(wide, 3), axis=0).astype(BF16)
        for tiles, directions in (((5, 6), (4, 5)), ((2, 3), (2, 3)), ((0, 1), (0, 1)), ((4,), ())):
            low = LANES * tiles[0]
            spread = dot(split, pick_t[:, low : low + LANES * len(tiles)])
            spread = spread[0:40] + spread[40:80] + spread[80:120]
            for n, t in enumerate(tiles):
                part[step, t] = spread[:, LANES * n : LANES * (n + 1)]
            send_halo(step, directions)

    def own(tiles):
        return [x if t == 4 else jnp.where(own_half, x, 0.0) for t, x in enumerate(tiles)]

    def product(mine, tiles):
        total = mine[0] * tiles[0]
        for t in range(1, 7):
            total = total + mine[t] * tiles[t]
        return jnp.sum(total, axis=0, keepdims=True)

    def energy_row(energy):
        row = jnp.sum(energy, axis=0, keepdims=True)
        return row[:, 0:128] + row[:, 128:256]

    def to_lanes(lines):
        square = jnp.concatenate(lines + [jnp.zeros((16 - len(lines), LANES), F32)], axis=0)
        sums = jnp.sum(square, axis=1, keepdims=True)
        on_diagonal = lax.broadcasted_iota(jnp.int32, (16, LANES), 0) == lax.broadcasted_iota(jnp.int32, (16, LANES), 1)
        return jnp.sum(jnp.where(on_diagonal, sums, 0.0), axis=0, keepdims=True)

    def scalar(line, q):
        return jnp.broadcast_to(line[:, q : q + 1], (1, LANES))

    def combine(terms):
        total = None
        for factor, value in terms:
            total = factor * value if total is None else total + factor * value
        return total

    def back(tiles_list):
        stack = []
        for tiles in tiles_list:
            stack += pieces(jnp.concatenate(tiles, axis=1), 3)
        moved = dot_nt(jnp.concatenate(stack, axis=0).astype(BF16), place[...])
        out = []
        for i in range(len(tiles_list)):
            out.append(moved[120 * i : 120 * i + 40] + moved[120 * i + 40 : 120 * i + 80] + moved[120 * i + 80 : 120 * i + 120])
        return out

    total = blocks_ref[...]
    total = jnp.sum(total * total, axis=(0, 1, 2))
    rho = 1.0 + jnp.sum(total.reshape(1, 6400), axis=1, keepdims=True) * (3.0 / 160.0)
    rho = jnp.broadcast_to(rho, (1, LANES))
    theta = 256.0 * rho
    inv_theta = 1.0 / theta
    keep = (1.0 - rho) * inv_theta

    basis, masked, sums, moved = [], [], {}, [rhs]

    def advance(step):
        def tile(t, got):
            return got if step == 0 else keep * basis[-1][t] + inv_theta * got

        early = [tile(k, receive(step, k)) for k in range(4)] + [tile(4, part[step, 4])]
        picked = gather(early, 0, EARLY) if step < 4 else None
        late = [tile(TILE[k], receive(step, k)) for k in (4, 5)]
        if step < 4:
            picked = picked + gather(late, EARLY, 896)
        basis.append(early + late)
        return picked

    def add_inner(i, j):
        sums[i, j] = product(masked[i], basis[j])

    for step in range(3):
        if step == 1:
            pl.semaphore_wait(near_sem, 4)
            tell(far_sem, along("gz", 4, 12) + along("gy", 1, 2, 3))
        picked = advance(step)
        if step == 0:
            tell(near_sem, along("gz", 2, 14) + along("gx", 2, 6))
        project(picked, False)
        masked.append(own(basis[step]))
        scatter(step + 1)
        for i in range(step + 1):
            add_inner(i, step)
        if step:
            moved += back([basis[step]])
    energy = project(advance(3), True)
    masked.append(own(basis[3]))
    for i in range(4):
        add_inner(i, 3)
    pairs = [(i, j) for i in range(4) for j in range(i, 4)]
    pl.semaphore_wait(far_sem, 5)
    start_plane(0, to_lanes([sums[pair] for pair in pairs] + [sums[3, 3] + energy_row(energy)]))
    scatter(4)
    plane_to_line(0)
    moved += back([basis[3]])
    advance(4)
    moved += back([basis[4]])
    totals = finish_line(0)

    gram = {}
    for q, (i, j) in enumerate(pairs):
        gram[i, j] = gram[j, i] = scalar(totals, q)
    gram[3, 4] = (scalar(totals, len(pairs)) - rho * gram[3, 3]) * inv_theta
    gram[2, 4] = gram[3, 3]
    gram[1, 4] = gram[2, 3]
    gram[0, 4] = gram[1, 3]

    def apply(p):
        out = [rho * p[0]]
        for i in range(1, len(p)):
            out.append(rho * p[i] + theta * p[i - 1])
        return out + [theta * p[-1]]

    def form(a, b):
        return combine([(x, combine([(y, gram[i, j]) for j, y in enumerate(b)])) for i, x in enumerate(a)])

    norm = gram[0, 0]
    zero = jnp.zeros((1, LANES), F32)
    sol, res, direction = [zero] * 4, [zero + 1.0], [zero + 1.0]
    for i in range(4):
        image = apply(direction)
        alpha = norm / form(direction, image)
        for j, x in enumerate(direction):
            sol[j] = sol[j] + alpha * x
        res = [x - alpha * y for x, y in zip(res + [zero], image)]
        if i < 3:
            new = form(res, res)
            beta = new / norm
            direction = [x + beta * y for x, y in zip(res, direction + [zero])]
            norm = new

    def wide(line):
        return jnp.concatenate([line] * 4, axis=1)

    out_ref[0, :, 0, 0, :] = combine([(wide(c), x) for c, x in zip(sol, moved)])
    out_ref[1, :, 0, 0, :] = combine([(wide(c), x) for c, x in zip(res, moved)])
    for copy in sends:
        copy.wait_send()
    wait_all(plane_buf, plane_send, 0, PLANE - 1)
    wait_all(line_buf, line_send, 0, N_GZ - 1)


def local(right_side, elem_faces, elem_class, elem_scale, stretch, pml_flag, send_faces, blocks):
    vmem = pl.BlockSpec(memory_space=pltpu.VMEM)
    fields = jax.ShapeDtypeStruct((2, *right_side.shape), F32)
    given = (right_side, elem_faces, elem_class, elem_scale, stretch, pml_flag, send_faces, blocks)
    both = pl.pallas_call(
        kernel,
        out_shape=fields,
        in_specs=[pl.BlockSpec(memory_space=pl.ANY)] * len(given),
        out_specs=vmem,
        scratch_shapes=[pltpu.VMEM(x.shape, x.dtype) for x in given]
        + [
            pltpu.VMEM((120, 640), F32),
            pltpu.VMEM((256, 1024), BF16),
            pltpu.VMEM((512, 896), BF16),
            pltpu.VMEM((896, 1024), BF16),
            pltpu.VMEM((1024, 896), BF16),
            pltpu.VMEM((1024, 512), F32),
            pltpu.VMEM((960, 512), BF16),
            pltpu.VMEM((320, 1024), BF16),
            pltpu.VMEM((960, LANES), F32),
            pltpu.VMEM((1024, 256), BF16),
            pltpu.VMEM((1024, 256), BF16),
            pltpu.VMEM((STEPS, 7, 40, LANES), F32),
            pltpu.VMEM((STEPS, 6, 40, LANES), F32),
            pltpu.VMEM((1, PLANE, 1, LANES), F32),
            pltpu.VMEM((1, N_GZ, 1, LANES), F32),
            pltpu.SemaphoreType.DMA((STEPS, 6)),
            pltpu.SemaphoreType.DMA((STEPS, 6)),
            pltpu.SemaphoreType.DMA((1,)),
            pltpu.SemaphoreType.DMA((1,)),
            pltpu.SemaphoreType.DMA((1,)),
            pltpu.SemaphoreType.DMA((1,)),
            pltpu.SemaphoreType.DMA((len(given),)),
            pltpu.SemaphoreType.REGULAR,
            pltpu.SemaphoreType.REGULAR,
        ],
        compiler_params=pltpu.CompilerParams(
            collective_id=0, has_side_effects=True, vmem_limit_bytes=56 * 1024 * 1024
        ),
    )(*given)
    return both[0], both[1]


def solution(mesh):
    in_specs = (
        P(None, "gx", "gy", "gz"),
        P(None, "gx", "gy", "gz"),
        P("gx", "gy", "gz"),
        P("gx", "gy", "gz"),
        P(None, "gx", "gy", "gz"),
        P("gx", "gy", "gz"),
        P(None, "gx", "gy", "gz"),
        P(),
    )
    out_specs = (P(None, "gx", "gy", "gz"), P(None, "gx", "gy", "gz"))
    return jax.shard_map(local, mesh=mesh, in_specs=in_specs, out_specs=out_specs, check_vma=False)
```

```python
import functools

import jax
import jax.numpy as jnp
import numpy as np
from jax import lax
from jax.experimental import pallas as pl
from jax.experimental.pallas import tpu as pltpu
from jax.sharding import PartitionSpec as P

MESH = pl.DeviceIdType.MESH
F32 = jnp.float32
BF16 = jnp.bfloat16
N_GX, N_GY, N_GZ = 8, 4, 16
AXES = (("gx", N_GX), ("gy", N_GY), ("gz", N_GZ))
PLANE = N_GX * N_GY
LANES = 128
EARLY = 640
TILE = (0, 1, 2, 3, 5, 6)
STEPS = 5


def dot(a, b):
    return jnp.dot(a, b, preferred_element_type=F32)


def dot_nt(a, b):
    return lax.dot_general(a, b, (((1,), (1,)), ((), ())), preferred_element_type=F32)


def pieces(value, count):
    out = []
    for _ in range(count):
        head = value.astype(BF16).astype(F32)
        out.append(head)
        value = value - head
    return out


def onehot(left, right):
    return jnp.where(left == right, 1.0, 0.0).astype(BF16)


def embed_rows():
    column = lax.broadcasted_iota(jnp.int32, (1, 1024), 1)
    part, inside = column // 512, column % 512
    copy, place = inside // 160, inside % 160
    face, rest = place // 40, place % 40
    row = face * 20 + rest % 20 + jnp.where(copy == 2, 128, 0)
    return jnp.where((copy < 3) & (rest // 20 == part), row, -1)


def kernel(
    rhs_in,
    faces_in,
    class_in,
    scale_in,
    stretch_in,
    flag_in,
    send_in,
    blocks_in,
    out_ref,
    rhs_ref,
    faces_ref,
    class_ref,
    scale_ref,
    stretch_ref,
    flag_ref,
    send_ref,
    blocks_ref,
    lines640,
    embed,
    place,
    pick,
    pick_t,
    raw,
    smat,
    smat_t,
    rows,
    zhi,
    zlo,
    part,
    inbox,
    plane_buf,
    line_buf,
    halo_send,
    halo_recv,
    plane_send,
    plane_recv,
    line_send,
    line_recv,
    load_sem,
    near_sem,
    far_sem,
):
    at = {name: lax.axis_index(name) for name, _ in AXES}
    size = dict(AXES)

    def device(**moved):
        return tuple(moved.get(name, at[name]) for name, _ in AXES)

    neighbours, exists = [], []
    for name, n in AXES:
        neighbours.append(device(**{name: lax.rem(at[name] + (n - 1), n)}))
        neighbours.append(device(**{name: lax.rem(at[name] + 1, n)}))
        exists.append(at[name] > 0)
        exists.append(at[name] < n - 1)
    plane_at = at["gx"] * N_GY + at["gy"]
    offsets = [(dx, dy) for dx in range(N_GX) for dy in range(N_GY) if dx or dy]
    offsets.sort(key=lambda d: -(min(d[0], N_GX - d[0]) // 2 + min(d[1], N_GY - d[1])))
    plane_devices = []
    for dx, dy in offsets:
        plane_devices.append(device(gx=lax.rem(at["gx"] + dx, N_GX), gy=lax.rem(at["gy"] + dy, N_GY)))
    line_devices = []
    for step in sorted(range(1, N_GZ), key=lambda d: -min(d, N_GZ - d)):
        line_devices.append(device(gz=lax.rem(at["gz"] + step, N_GZ)))

    barrier = pltpu.get_barrier_semaphore()
    for other in neighbours:
        pl.semaphore_signal(barrier, inc=1, device_id=other, device_id_type=MESH)

    loads = []
    held = (send_ref, rhs_ref, faces_ref, blocks_ref, class_ref, scale_ref, stretch_ref, flag_ref)
    given = (send_in, rhs_in, faces_in, blocks_in, class_in, scale_in, stretch_in, flag_in)
    for i, (there, here) in enumerate(zip(given, held)):
        copy = pltpu.make_async_copy(there, here, load_sem.at[i])
        copy.start()
        loads.append(copy)

    def tell(sem, others):
        for other in others:
            pl.semaphore_signal(sem, inc=1, device_id=other, device_id_type=MESH)

    def along(name, *steps):
        return [device(**{name: lax.rem(at[name] + step, size[name])}) for step in steps]

    sends = []

    def send_halo(step, directions):
        for k in directions:
            copy = pltpu.make_async_remote_copy(
                src_ref=part.at[step, TILE[k]],
                dst_ref=inbox.at[step, k ^ 1],
                send_sem=halo_send.at[step, k],
                recv_sem=halo_recv.at[step, k ^ 1],
                device_id=neighbours[k],
                device_id_type=MESH,
            )
            copy.start()
            sends.append(copy)

    lane40 = lax.broadcasted_iota(jnp.int32, (40, LANES), 1)
    own_half = lane40 < 64

    def receive(step, k):
        pltpu.make_async_copy(inbox.at[step, k], inbox.at[step, k], halo_recv.at[step, k]).wait()
        mine, got = part[step, TILE[k]], pltpu.roll(inbox[step, k], 64, 1)
        return jnp.where(exists[k], mine + got, jnp.where(own_half, mine, 0.0))

    def start_sum(buf, send_sem, recv_sem, which, slot, others, value):
        buf[which, pl.ds(slot, 1)] = value[None]
        for other in others:
            pltpu.make_async_remote_copy(
                src_ref=buf.at[which, pl.ds(slot, 1)],
                dst_ref=buf.at[which, pl.ds(slot, 1)],
                send_sem=send_sem.at[which],
                recv_sem=recv_sem.at[which],
                device_id=other,
                device_id_type=MESH,
            ).start()

    def wait_all(buf, sem, which, count):
        some = buf.at[which, pl.ds(0, count)]
        pltpu.make_async_copy(some, some, sem.at[which]).wait()

    def start_plane(which, value):
        start_sum(plane_buf, plane_send, plane_recv, which, plane_at, plane_devices, value)

    def plane_to_line(which):
        wait_all(plane_buf, plane_recv, which, PLANE - 1)
        value = jnp.sum(plane_buf[which], axis=0)
        start_sum(line_buf, line_send, line_recv, which, at["gz"], line_devices, value)

    def finish_line(which):
        wait_all(line_buf, line_recv, which, N_GZ - 1)
        return jnp.sum(line_buf[which], axis=0)

    face512 = lax.broadcasted_iota(jnp.int32, (512, LANES), 0)
    no_face = jnp.full((1, 64), -1, jnp.int32)
    loads[0].wait()
    for k in range(6):
        shared = jnp.concatenate([send_ref[k, 0], no_face], axis=1)
        place[:, LANES * TILE[k] : LANES * (TILE[k] + 1)] = onehot(face512, shared)
    loads[1].wait()
    rhs = jnp.concatenate([rhs_ref[pl.ds(c, 40, stride=4), :] for c in range(4)], axis=1)
    rhs_split = jnp.concatenate(pieces(rhs, 3), axis=0).astype(BF16)

    def put(low, high):
        placed = dot(rhs_split, place[:, LANES * low : LANES * high])
        placed = placed[0:40] + placed[40:80] + placed[80:120]
        for t in range(low, high):
            part[0, t] = placed[:, LANES * (t - low) : LANES * (t - low + 1)]

    put(5, 7)
    put(0, 4)
    pl.semaphore_wait(barrier, 6)
    send_halo(0, (4, 5, 2, 3, 0, 1))

    position = lax.broadcasted_iota(jnp.int32, (1, 384), 1)
    target = ((position // 64) * 128 + jnp.where(position >= 256, 128, 0) + position % 64 + 1).astype(F32)
    face_col = lax.broadcasted_iota(jnp.int32, (512, 1), 0)
    sent = jnp.concatenate([send_ref[k, 0] for k in range(6)], axis=1)
    found = jnp.sum(jnp.where(face_col == sent, target, 0.0), axis=1, keepdims=True)
    inner = jnp.broadcast_to(jnp.where(found > 0.0, 0.0, 1.0), (512, LANES)).astype(BF16)
    below = jnp.where(
        lax.broadcasted_iota(jnp.int32, (512, 512), 1) < lax.broadcasted_iota(jnp.int32, (512, 512), 0), 1.0, 0.0
    ).astype(BF16)
    rank = dot(below, inner)
    new_place = jnp.where(jnp.broadcast_to(found, (512, LANES)) > 0.0, found - 1.0, 512.0 + rank)
    lane512 = lax.broadcasted_iota(jnp.int32, (512, LANES), 1)
    place[:, 512:640] = onehot(new_place.astype(jnp.int32), lane512 + 512)
    put(4, 5)

    place_row = new_place.T[0:8, :]
    high = jnp.floor(place_row * (1.0 / 32.0))
    digits = jnp.concatenate([high, place_row - 32.0 * high], axis=0).astype(BF16)
    row512 = lax.broadcasted_iota(jnp.int32, (512, 256), 0)
    row128 = lax.broadcasted_iota(jnp.int32, (LANES, 256), 0)
    lane256 = lax.broadcasted_iota(jnp.int32, (256, LANES), 1)
    loads[2].wait()
    for f in range(4):
        old = faces_ref[f, 0]
        looked = dot(digits, onehot(row512, old))
        owned = (looked[0:1] * 32.0 + looked[8:9]).astype(jnp.int32)
        slot = old - 512
        new = jnp.where(old < 512, owned, (slot // 64) * 128 + jnp.where(slot >= 256, 128, 0) + 64 + slot % 64)
        for t in range(7):
            pick[LANES * t : LANES * (t + 1), 256 * f : 256 * (f + 1)] = onehot(row128 + LANES * t, new)
        column = jnp.broadcast_to(new.astype(F32), (LANES, 256)).T.astype(jnp.int32)
        for t in range(7):
            pick_t[256 * f : 256 * (f + 1), LANES * t : LANES * (t + 1)] = onehot(column, lane256 + LANES * t)

    embed[...] = onehot(lax.broadcasted_iota(jnp.int32, (256, 1024), 0), embed_rows())
    loads[3].wait()
    for b in range(6):
        for g in range(10):
            lines640[20 * b + 2 * g : 20 * b + 2 * g + 2, :] = blocks_ref[b // 3, b % 3, :, 640 * g : 640 * g + 640]
    for k in range(8):
        piece = lines640[:, 80 * k : 80 * k + 80]
        rows[pl.ds(k, 120, stride=8), :] = jnp.concatenate([piece, jnp.zeros((120, 48), F32)], axis=1)
    for b in range(6):
        both = jnp.concatenate(pieces(rows[160 * b : 160 * b + 160, :], 2), axis=1).astype(BF16)
        spread = dot(both, embed[...]).reshape(10, 2, 8, 1024)
        real, imag = spread[:, 0].reshape(80, 1024), spread[:, 1].reshape(80, 1024)
        block = jnp.concatenate([real[:, :512] - imag[:, 512:], imag[:, :512] + real[:, 512:]], axis=0)
        raw[160 * b : 160 * b + 160, :] = block
        smat[160 * b : 160 * b + 160, :] = block.astype(BF16)
    raw[960:1024, :] = jnp.zeros((64, 512), F32)
    smat_t[0:160, :] = raw[:, 0:256].T[0:160].astype(BF16)
    smat_t[160:320, :] = raw[:, 256:512].T[64:224].astype(BF16)
    zhi[960:1024, :] = jnp.zeros((64, 256), BF16)
    zlo[960:1024, :] = jnp.zeros((64, 256), BF16)
    for copy in loads[4:]:
        copy.wait()
    weights = []
    for c in range(2):
        for d in range(3):
            factor = jnp.where(flag_ref[0] > 0, stretch_ref[d, 0], 1.0)
            weights.append(jnp.where(class_ref[0] == c, scale_ref[0] * factor, 0.0))

    def gather(tiles, low, high):
        split = pieces(jnp.concatenate(tiles, axis=1), 2)
        return dot(jnp.concatenate(split, axis=0).astype(BF16), pick[low:high, :])

    def project(picked, with_energy):
        upper = [picked[0:40, 256 * f : 256 * f + 256] for f in range(4)]
        lower = [picked[40:80, 256 * f : 256 * f + 256] for f in range(4)]
        stacked = jnp.concatenate(upper + lower + upper + [jnp.zeros((32, 256), F32)], axis=0).astype(BF16)
        energy = jnp.zeros((8, 256), F32)
        for b in range(6):
            projected = dot(smat[160 * b : 160 * b + 160, :], stacked)
            weighted = projected * weights[b]
            if with_energy:
                energy = energy + jnp.sum((weighted * projected).reshape(20, 8, 256), axis=0)
            head, tail = pieces(weighted, 2)
            zhi[160 * b : 160 * b + 160, :] = head.astype(BF16)
            zlo[160 * b : 160 * b + 160, :] = tail.astype(BF16)
        return energy

    def scatter(step):
        both = dot(smat_t[...], zhi[...])
        image = both[0:160] + both[160:320] + dot(smat_t[0:160, :], zlo[...])
        wide = jnp.concatenate([image[40 * f : 40 * f + 40] for f in range(4)], axis=1)
        split = jnp.concatenate(pieces(wide, 3), axis=0).astype(BF16)
        for tiles, directions in (((5, 6), (4, 5)), ((2, 3), (2, 3)), ((0, 1), (0, 1)), ((4,), ())):
            low = LANES * tiles[0]
            spread = dot(split, pick_t[:, low : low + LANES * len(tiles)])
            spread = spread[0:40] + spread[40:80] + spread[80:120]
            for n, t in enumerate(tiles):
                part[step, t] = spread[:, LANES * n : LANES * (n + 1)]
            send_halo(step, directions)

    def own(tiles):
        return [x if t == 4 else jnp.where(own_half, x, 0.0) for t, x in enumerate(tiles)]

    def product(mine, tiles):
        total = mine[0] * tiles[0]
        for t in range(1, 7):
            total = total + mine[t] * tiles[t]
        return jnp.sum(total, axis=0, keepdims=True)

    def energy_row(energy):
        row = jnp.sum(energy, axis=0, keepdims=True)
        return row[:, 0:128] + row[:, 128:256]

    def to_lanes(lines):
        square = jnp.concatenate(lines + [jnp.zeros((16 - len(lines), LANES), F32)], axis=0)
        sums = jnp.sum(square, axis=1, keepdims=True)
        on_diagonal = lax.broadcasted_iota(jnp.int32, (16, LANES), 0) == lax.broadcasted_iota(jnp.int32, (16, LANES), 1)
        return jnp.sum(jnp.where(on_diagonal, sums, 0.0), axis=0, keepdims=True)

    def scalar(line, q):
        return jnp.broadcast_to(line[:, q : q + 1], (1, LANES))

    def combine(terms):
        total = None
        for factor, value in terms:
            total = factor * value if total is None else total + factor * value
        return total

    def back(tiles_list):
        stack = []
        for tiles in tiles_list:
            stack += pieces(jnp.concatenate(tiles, axis=1), 3)
        moved = dot_nt(jnp.concatenate(stack, axis=0).astype(BF16), place[...])
        out = []
        for i in range(len(tiles_list)):
            out.append(moved[120 * i : 120 * i + 40] + moved[120 * i + 40 : 120 * i + 80] + moved[120 * i + 80 : 120 * i + 120])
        return out

    total = blocks_ref[...]
    total = jnp.sum(total * total, axis=(0, 1, 2))
    rho = 1.0 + jnp.sum(total.reshape(1, 6400), axis=1, keepdims=True) * (3.0 / 160.0)
    rho = jnp.broadcast_to(rho, (1, LANES))
    theta = 256.0 * rho
    inv_theta = 1.0 / theta
    keep = (1.0 - rho) * inv_theta

    basis, masked, sums, moved = [], [], {}, [rhs]

    def advance(step):
        def tile(t, got):
            return got if step == 0 else keep * basis[-1][t] + inv_theta * got

        early = [tile(k, receive(step, k)) for k in range(4)] + [tile(4, part[step, 4])]
        picked = gather(early, 0, EARLY) if step < 4 else None
        late = [tile(TILE[k], receive(step, k)) for k in (4, 5)]
        if step < 4:
            picked = picked + gather(late, EARLY, 896)
        basis.append(early + late)
        return picked

    def add_inner(i, j):
        sums[i, j] = product(masked[i], basis[j])

    for step in range(3):
        if step == 1:
            pl.semaphore_wait(near_sem, 4)
            tell(far_sem, along("gz", 4, 12) + along("gy", 1, 2, 3))
        picked = advance(step)
        if step == 0:
            tell(near_sem, along("gz", 2, 14) + along("gx", 2, 6))
        project(picked, False)
        masked.append(own(basis[step]))
        scatter(step + 1)
        for i in range(step + 1):
            add_inner(i, step)
        if step:
            moved += back([basis[step]])
    energy = project(advance(3), True)
    masked.append(own(basis[3]))
    for i in range(4):
        add_inner(i, 3)
    pairs = [(i, j) for i in range(4) for j in range(i, 4)]
    pl.semaphore_wait(far_sem, 5)
    start_plane(0, to_lanes([sums[pair] for pair in pairs] + [sums[3, 3] + energy_row(energy)]))
    scatter(4)
    plane_to_line(0)
    moved += back([basis[3]])
    advance(4)
    moved += back([basis[4]])
    totals = finish_line(0)

    gram = {}
    for q, (i, j) in enumerate(pairs):
        gram[i, j] = gram[j, i] = scalar(totals, q)
    gram[3, 4] = (scalar(totals, len(pairs)) - rho * gram[3, 3]) * inv_theta
    gram[2, 4] = gram[3, 3]
    gram[1, 4] = gram[2, 3]
    gram[0, 4] = gram[1, 3]

    work = {(i, j): theta * gram[i, j + 1] + rho * gram[i, j] for i, j in pairs}
    right = [gram[0, i] for i in range(4)]
    factor, inverse = {}, []
    for i in range(4):
        inverse.append(1.0 / work[i, i])
        for j in range(i + 1, 4):
            factor[i, j] = work[i, j] * inverse[i]
        for j in range(i + 1, 4):
            for k in range(j, 4):
                work[j, k] = work[j, k] - factor[i, j] * work[i, k]
            right[j] = right[j] - factor[i, j] * right[i]
    sol = [right[i] * inverse[i] for i in range(4)]
    for i in reversed(range(4)):
        for j in range(i):
            sol[j] = sol[j] - factor[j, i] * sol[i]
    res = [1.0 - rho * sol[0]]
    for i in range(1, 4):
        res.append(-(rho * sol[i] + theta * sol[i - 1]))
    res.append(-theta * sol[3])

    def wide(line):
        return jnp.concatenate([line] * 4, axis=1)

    for base, factors in ((0, sol), (160, res)):
        value = combine([(wide(c), x) for c, x in zip(factors, moved)])
        for c in range(4):
            out_ref[pl.ds(base + c, 40, stride=4), :] = value[:, LANES * c : LANES * (c + 1)]
    for copy in sends:
        copy.wait_send()
    wait_all(plane_buf, plane_send, 0, PLANE - 1)
    wait_all(line_buf, line_send, 0, N_GZ - 1)


def local(right_side, elem_faces, elem_class, elem_scale, stretch, pml_flag, send_faces, blocks):
    vmem = pl.BlockSpec(memory_space=pltpu.VMEM)
    fields = jax.ShapeDtypeStruct((320, LANES), F32)
    given = (right_side.reshape(160, LANES), elem_faces, elem_class, elem_scale, stretch, pml_flag, send_faces, blocks)
    both = pl.pallas_call(
        kernel,
        out_shape=fields,
        in_specs=[pl.BlockSpec(memory_space=pl.ANY)] * len(given),
        out_specs=vmem,
        scratch_shapes=[pltpu.VMEM(x.shape, x.dtype) for x in given]
        + [
            pltpu.VMEM((120, 640), F32),
            pltpu.VMEM((256, 1024), BF16),
            pltpu.VMEM((512, 896), BF16),
            pltpu.VMEM((896, 1024), BF16),
            pltpu.VMEM((1024, 896), BF16),
            pltpu.VMEM((1024, 512), F32),
            pltpu.VMEM((960, 512), BF16),
            pltpu.VMEM((320, 1024), BF16),
            pltpu.VMEM((960, LANES), F32),
            pltpu.VMEM((1024, 256), BF16),
            pltpu.VMEM((1024, 256), BF16),
            pltpu.VMEM((STEPS, 7, 40, LANES), F32),
            pltpu.VMEM((STEPS, 6, 40, LANES), F32),
            pltpu.VMEM((1, PLANE, 1, LANES), F32),
            pltpu.VMEM((1, N_GZ, 1, LANES), F32),
            pltpu.SemaphoreType.DMA((STEPS, 6)),
            pltpu.SemaphoreType.DMA((STEPS, 6)),
            pltpu.SemaphoreType.DMA((1,)),
            pltpu.SemaphoreType.DMA((1,)),
            pltpu.SemaphoreType.DMA((1,)),
            pltpu.SemaphoreType.DMA((1,)),
            pltpu.SemaphoreType.DMA((len(given),)),
            pltpu.SemaphoreType.REGULAR,
            pltpu.SemaphoreType.REGULAR,
        ],
        compiler_params=pltpu.CompilerParams(
            collective_id=0, has_side_effects=True, vmem_limit_bytes=40 * 1024 * 1024
        ),
    )(*[pltpu.with_memory_space_constraint(x, pltpu.HBM) for x in given])
    return both[:160].reshape(right_side.shape), both[160:].reshape(right_side.shape)


def solution(mesh):
    in_specs = (
        P(None, "gx", "gy", "gz"),
        P(None, "gx", "gy", "gz"),
        P("gx", "gy", "gz"),
        P("gx", "gy", "gz"),
        P(None, "gx", "gy", "gz"),
        P("gx", "gy", "gz"),
        P(None, "gx", "gy", "gz"),
        P(),
    )
    out_specs = (P(None, "gx", "gy", "gz"), P(None, "gx", "gy", "gz"))
    return jax.shard_map(local, mesh=mesh, in_specs=in_specs, out_specs=out_specs, check_vma=False)
```

```python
import functools

import jax
import jax.numpy as jnp
import numpy as np
from jax import lax
from jax.experimental import pallas as pl
from jax.experimental.pallas import tpu as pltpu
from jax.sharding import PartitionSpec as P

MESH = pl.DeviceIdType.MESH
F32 = jnp.float32
BF16 = jnp.bfloat16
N_GX, N_GY, N_GZ = 8, 4, 16
AXES = (("gx", N_GX), ("gy", N_GY), ("gz", N_GZ))
PLANE = N_GX * N_GY
LANES = 128
EARLY = 640
TILE = (0, 1, 2, 3, 5, 6)
STEPS = 5


def dot(a, b):
    return jnp.dot(a, b, preferred_element_type=F32)


def dot_nt(a, b):
    return lax.dot_general(a, b, (((1,), (1,)), ((), ())), preferred_element_type=F32)


def pieces(value, count):
    out = []
    for _ in range(count):
        head = value.astype(BF16).astype(F32)
        out.append(head)
        value = value - head
    return out


def onehot(left, right):
    return jnp.where(left == right, 1.0, 0.0).astype(BF16)


def embed_rows():
    column = lax.broadcasted_iota(jnp.int32, (1, 1024), 1)
    part, inside = column // 512, column % 512
    copy, place = inside // 160, inside % 160
    face, rest = place // 40, place % 40
    row = face * 20 + rest % 20 + jnp.where(copy == 2, 128, 0)
    return jnp.where((copy < 3) & (rest // 20 == part), row, -1)


def kernel(
    rhs_in,
    faces_in,
    class_in,
    scale_in,
    stretch_in,
    flag_in,
    send_in,
    blocks_in,
    out_ref,
    rhs_ref,
    faces_ref,
    class_ref,
    scale_ref,
    stretch_ref,
    flag_ref,
    send_ref,
    blocks_ref,
    lines640,
    embed,
    place,
    pick,
    pick_t,
    raw,
    smat,
    smat_t,
    rows,
    zhi,
    zlo,
    part,
    inbox,
    plane_buf,
    line_buf,
    halo_send,
    halo_recv,
    plane_send,
    plane_recv,
    line_send,
    line_recv,
    load_sem,
    near_sem,
    far_sem,
):
    at = {name: lax.axis_index(name) for name, _ in AXES}
    size = dict(AXES)

    def device(**moved):
        return tuple(moved.get(name, at[name]) for name, _ in AXES)

    neighbours, exists = [], []
    for name, n in AXES:
        neighbours.append(device(**{name: lax.rem(at[name] + (n - 1), n)}))
        neighbours.append(device(**{name: lax.rem(at[name] + 1, n)}))
        exists.append(at[name] > 0)
        exists.append(at[name] < n - 1)
    plane_at = at["gx"] * N_GY + at["gy"]
    offsets = [(dx, dy) for dx in range(N_GX) for dy in range(N_GY) if dx or dy]
    offsets.sort(key=lambda d: -(min(d[0], N_GX - d[0]) // 2 + min(d[1], N_GY - d[1])))
    plane_devices = []
    for dx, dy in offsets:
        plane_devices.append(device(gx=lax.rem(at["gx"] + dx, N_GX), gy=lax.rem(at["gy"] + dy, N_GY)))
    line_devices = []
    for step in sorted(range(1, N_GZ), key=lambda d: -min(d, N_GZ - d)):
        line_devices.append(device(gz=lax.rem(at["gz"] + step, N_GZ)))

    barrier = pltpu.get_barrier_semaphore()
    for other in reversed(neighbours):
        pl.semaphore_signal(barrier, inc=1, device_id=other, device_id_type=MESH)

    loads = []
    held = (send_ref, rhs_ref, faces_ref, blocks_ref, class_ref, scale_ref, stretch_ref, flag_ref)
    given = (send_in, rhs_in, faces_in, blocks_in, class_in, scale_in, stretch_in, flag_in)
    for i, (there, here) in enumerate(zip(given, held)):
        copy = pltpu.make_async_copy(there, here, load_sem.at[i])
        copy.start()
        loads.append(copy)

    def tell(sem, others):
        for other in others:
            pl.semaphore_signal(sem, inc=1, device_id=other, device_id_type=MESH)

    def along(name, *steps):
        return [device(**{name: lax.rem(at[name] + step, size[name])}) for step in steps]

    sends = []

    def send_halo(step, directions):
        for k in directions:
            copy = pltpu.make_async_remote_copy(
                src_ref=part.at[step, TILE[k]],
                dst_ref=inbox.at[step, k ^ 1],
                send_sem=halo_send.at[step, k],
                recv_sem=halo_recv.at[step, k ^ 1],
                device_id=neighbours[k],
                device_id_type=MESH,
            )
            copy.start()
            sends.append(copy)

    lane40 = lax.broadcasted_iota(jnp.int32, (40, LANES), 1)
    own_half = lane40 < 64

    def receive(step, k):
        pltpu.make_async_copy(inbox.at[step, k], inbox.at[step, k], halo_recv.at[step, k]).wait()
        mine, got = part[step, TILE[k]], pltpu.roll(inbox[step, k], 64, 1)
        return jnp.where(exists[k], mine + got, jnp.where(own_half, mine, 0.0))

    def start_sum(buf, send_sem, recv_sem, which, slot, others, value):
        buf[which, pl.ds(slot, 1)] = value[None]
        for other in others:
            pltpu.make_async_remote_copy(
                src_ref=buf.at[which, pl.ds(slot, 1)],
                dst_ref=buf.at[which, pl.ds(slot, 1)],
                send_sem=send_sem.at[which],
                recv_sem=recv_sem.at[which],
                device_id=other,
                device_id_type=MESH,
            ).start()

    def wait_all(buf, sem, which, count):
        some = buf.at[which, pl.ds(0, count)]
        pltpu.make_async_copy(some, some, sem.at[which]).wait()

    def start_plane(which, value):
        start_sum(plane_buf, plane_send, plane_recv, which, plane_at, plane_devices, value)

    def plane_to_line(which):
        wait_all(plane_buf, plane_recv, which, PLANE - 1)
        value = jnp.sum(plane_buf[which], axis=0)
        start_sum(line_buf, line_send, line_recv, which, at["gz"], line_devices, value)

    def finish_line(which):
        wait_all(line_buf, line_recv, which, N_GZ - 1)
        return jnp.sum(line_buf[which], axis=0)

    face512 = lax.broadcasted_iota(jnp.int32, (512, LANES), 0)
    no_face = jnp.full((1, 64), -1, jnp.int32)
    loads[0].wait()
    for k in range(6):
        shared = jnp.concatenate([send_ref[k, 0], no_face], axis=1)
        place[:, LANES * TILE[k] : LANES * (TILE[k] + 1)] = onehot(face512, shared)
    loads[1].wait()
    rhs = jnp.concatenate([rhs_ref[pl.ds(c, 40, stride=4), :] for c in range(4)], axis=1)
    rhs_split = jnp.concatenate(pieces(rhs, 3), axis=0).astype(BF16)

    def put(low, high):
        placed = dot(rhs_split, place[:, LANES * low : LANES * high])
        placed = placed[0:40] + placed[40:80] + placed[80:120]
        for t in range(low, high):
            part[0, t] = placed[:, LANES * (t - low) : LANES * (t - low + 1)]

    put(5, 7)
    put(0, 4)
    pl.semaphore_wait(barrier, 6)
    send_halo(0, (4, 5, 2, 3, 0, 1))

    position = lax.broadcasted_iota(jnp.int32, (1, 384), 1)
    target = ((position // 64) * 128 + jnp.where(position >= 256, 128, 0) + position % 64 + 1).astype(F32)
    face_col = lax.broadcasted_iota(jnp.int32, (512, 1), 0)
    sent = jnp.concatenate([send_ref[k, 0] for k in range(6)], axis=1)
    found = jnp.sum(jnp.where(face_col == sent, target, 0.0), axis=1, keepdims=True)
    inner = jnp.broadcast_to(jnp.where(found > 0.0, 0.0, 1.0), (512, LANES)).astype(BF16)
    below = jnp.where(
        lax.broadcasted_iota(jnp.int32, (512, 512), 1) < lax.broadcasted_iota(jnp.int32, (512, 512), 0), 1.0, 0.0
    ).astype(BF16)
    rank = dot(below, inner)
    new_place = jnp.where(jnp.broadcast_to(found, (512, LANES)) > 0.0, found - 1.0, 512.0 + rank)
    lane512 = lax.broadcasted_iota(jnp.int32, (512, LANES), 1)
    place[:, 512:640] = onehot(new_place.astype(jnp.int32), lane512 + 512)
    put(4, 5)

    place_row = new_place.T[0:8, :]
    high = jnp.floor(place_row * (1.0 / 32.0))
    digits = jnp.concatenate([high, place_row - 32.0 * high], axis=0).astype(BF16)
    row512 = lax.broadcasted_iota(jnp.int32, (512, 256), 0)
    row128 = lax.broadcasted_iota(jnp.int32, (LANES, 256), 0)
    lane256 = lax.broadcasted_iota(jnp.int32, (256, LANES), 1)
    loads[2].wait()
    for f in range(4):
        old = faces_ref[f, 0]
        looked = dot(digits, onehot(row512, old))
        owned = (looked[0:1] * 32.0 + looked[8:9]).astype(jnp.int32)
        slot = old - 512
        new = jnp.where(old < 512, owned, (slot // 64) * 128 + jnp.where(slot >= 256, 128, 0) + 64 + slot % 64)
        for t in range(7):
            pick[LANES * t : LANES * (t + 1), 256 * f : 256 * (f + 1)] = onehot(row128 + LANES * t, new)
        column = jnp.broadcast_to(new.astype(F32), (LANES, 256)).T.astype(jnp.int32)
        for t in range(7):
            pick_t[256 * f : 256 * (f + 1), LANES * t : LANES * (t + 1)] = onehot(column, lane256 + LANES * t)

    embed[...] = onehot(lax.broadcasted_iota(jnp.int32, (256, 1024), 0), embed_rows())
    loads[3].wait()
    for b in range(6):
        for g in range(10):
            lines640[20 * b + 2 * g : 20 * b + 2 * g + 2, :] = blocks_ref[b // 3, b % 3, :, 640 * g : 640 * g + 640]
    for k in range(8):
        piece = lines640[:, 80 * k : 80 * k + 80]
        rows[pl.ds(k, 120, stride=8), :] = jnp.concatenate([piece, jnp.zeros((120, 48), F32)], axis=1)
    for b in range(6):
        both = jnp.concatenate(pieces(rows[160 * b : 160 * b + 160, :], 2), axis=1).astype(BF16)
        spread = dot(both, embed[...]).reshape(10, 2, 8, 1024)
        real, imag = spread[:, 0].reshape(80, 1024), spread[:, 1].reshape(80, 1024)
        block = jnp.concatenate([real[:, :512] - imag[:, 512:], imag[:, :512] + real[:, 512:]], axis=0)
        raw[160 * b : 160 * b + 160, :] = block
        smat[160 * b : 160 * b + 160, :] = block.astype(BF16)
    raw[960:1024, :] = jnp.zeros((64, 512), F32)
    smat_t[0:160, :] = raw[:, 0:256].T[0:160].astype(BF16)
    smat_t[160:320, :] = raw[:, 256:512].T[64:224].astype(BF16)
    zhi[960:1024, :] = jnp.zeros((64, 256), BF16)
    zlo[960:1024, :] = jnp.zeros((64, 256), BF16)
    for copy in loads[4:]:
        copy.wait()
    weights = []
    for c in range(2):
        for d in range(3):
            factor = jnp.where(flag_ref[0] > 0, stretch_ref[d, 0], 1.0)
            weights.append(jnp.where(class_ref[0] == c, scale_ref[0] * factor, 0.0))

    def gather(tiles, low, high):
        split = pieces(jnp.concatenate(tiles, axis=1), 2)
        return dot(jnp.concatenate(split, axis=0).astype(BF16), pick[low:high, :])

    def project(picked, with_energy):
        upper = [picked[0:40, 256 * f : 256 * f + 256] for f in range(4)]
        lower = [picked[40:80, 256 * f : 256 * f + 256] for f in range(4)]
        stacked = jnp.concatenate(upper + lower + upper + [jnp.zeros((32, 256), F32)], axis=0).astype(BF16)
        energy = jnp.zeros((8, 256), F32)
        for b in range(6):
            projected = dot(smat[160 * b : 160 * b + 160, :], stacked)
            weighted = projected * weights[b]
            if with_energy:
                energy = energy + jnp.sum((weighted * projected).reshape(20, 8, 256), axis=0)
            head, tail = pieces(weighted, 2)
            zhi[160 * b : 160 * b + 160, :] = head.astype(BF16)
            zlo[160 * b : 160 * b + 160, :] = tail.astype(BF16)
        return energy

    def scatter(step):
        both = dot(smat_t[...], zhi[...])
        image = both[0:160] + both[160:320] + dot(smat_t[0:160, :], zlo[...])
        wide = jnp.concatenate([image[40 * f : 40 * f + 40] for f in range(4)], axis=1)
        split = jnp.concatenate(pieces(wide, 3), axis=0).astype(BF16)
        for tiles, directions in (((5, 6), (4, 5)), ((2, 3), (2, 3)), ((0, 1), (0, 1)), ((4,), ())):
            low = LANES * tiles[0]
            spread = dot(split, pick_t[:, low : low + LANES * len(tiles)])
            spread = spread[0:40] + spread[40:80] + spread[80:120]
            for n, t in enumerate(tiles):
                part[step, t] = spread[:, LANES * n : LANES * (n + 1)]
            send_halo(step, directions)

    def own(tiles):
        return [x if t == 4 else jnp.where(own_half, x, 0.0) for t, x in enumerate(tiles)]

    def product(mine, tiles):
        total = mine[0] * tiles[0]
        for t in range(1, 7):
            total = total + mine[t] * tiles[t]
        return jnp.sum(total, axis=0, keepdims=True)

    def energy_row(energy):
        row = jnp.sum(energy, axis=0, keepdims=True)
        return row[:, 0:128] + row[:, 128:256]

    def to_lanes(lines):
        square = jnp.concatenate(lines + [jnp.zeros((16 - len(lines), LANES), F32)], axis=0)
        sums = jnp.sum(square, axis=1, keepdims=True)
        on_diagonal = lax.broadcasted_iota(jnp.int32, (16, LANES), 0) == lax.broadcasted_iota(jnp.int32, (16, LANES), 1)
        return jnp.sum(jnp.where(on_diagonal, sums, 0.0), axis=0, keepdims=True)

    def scalar(line, q):
        return jnp.broadcast_to(line[:, q : q + 1], (1, LANES))

    def combine(terms):
        total = None
        for factor, value in terms:
            total = factor * value if total is None else total + factor * value
        return total

    def back(tiles_list):
        stack = []
        for tiles in tiles_list:
            stack += pieces(jnp.concatenate(tiles, axis=1), 3)
        moved = dot_nt(jnp.concatenate(stack, axis=0).astype(BF16), place[...])
        out = []
        for i in range(len(tiles_list)):
            out.append(moved[120 * i : 120 * i + 40] + moved[120 * i + 40 : 120 * i + 80] + moved[120 * i + 80 : 120 * i + 120])
        return out

    total = blocks_ref[...]
    total = jnp.sum(total * total, axis=(0, 1, 2))
    rho = 1.0 + jnp.sum(total.reshape(1, 6400), axis=1, keepdims=True) * (3.0 / 160.0)
    rho = jnp.broadcast_to(rho, (1, LANES))
    theta = 256.0 * rho
    inv_theta = 1.0 / theta
    keep = (1.0 - rho) * inv_theta

    basis, masked, sums, moved = [], [], {}, [rhs]

    def advance(step):
        def tile(t, got):
            return got if step == 0 else keep * basis[-1][t] + inv_theta * got

        early = [tile(k, receive(step, k)) for k in range(4)] + [tile(4, part[step, 4])]
        picked = gather(early, 0, EARLY) if step < 4 else None
        late = [tile(TILE[k], receive(step, k)) for k in (4, 5)]
        if step < 4:
            picked = picked + gather(late, EARLY, 896)
        basis.append(early + late)
        return picked

    def add_inner(i, j):
        sums[i, j] = product(masked[i], basis[j])

    for step in range(3):
        if step == 1:
            pl.semaphore_wait(near_sem, 4)
            tell(far_sem, along("gz", 4, 12) + along("gy", 1, 2, 3))
        picked = advance(step)
        if step == 0:
            tell(near_sem, along("gz", 2, 14) + along("gx", 2, 6))
        project(picked, False)
        masked.append(own(basis[step]))
        scatter(step + 1)
        for i in range(step + 1):
            add_inner(i, step)
        if step:
            moved += back([basis[step]])
    picked = advance(3)
    pl.semaphore_wait(far_sem, 5)
    masked.append(own(basis[3]))
    for i in range(4):
        add_inner(i, 3)
    pairs = [(i, j) for i in range(4) for j in range(i, 4)]
    products = to_lanes([sums[pair] for pair in pairs] + [sums[3, 3]])
    energy = jnp.sum(energy_row(project(picked, True)), axis=1, keepdims=True)
    lane = lax.broadcasted_iota(jnp.int32, (1, LANES), 1)
    start_plane(0, products + jnp.where(lane == len(pairs), energy, 0.0))
    scatter(4)
    plane_to_line(0)
    moved += back([basis[3]])
    advance(4)
    moved += back([basis[4]])
    for copy in sends:
        copy.wait_send()
    wait_all(plane_buf, plane_send, 0, PLANE - 1)
    wait_all(line_buf, line_send, 0, N_GZ - 1)
    totals = finish_line(0)

    gram = {}
    for q, (i, j) in enumerate(pairs):
        gram[i, j] = gram[j, i] = scalar(totals, q)
    gram[3, 4] = (scalar(totals, len(pairs)) - rho * gram[3, 3]) * inv_theta
    gram[2, 4] = gram[3, 3]
    gram[1, 4] = gram[2, 3]
    gram[0, 4] = gram[1, 3]

    work = {(i, j): theta * gram[i, j + 1] + rho * gram[i, j] for i, j in pairs}
    right = [gram[0, i] for i in range(4)]
    factor, inverse = {}, []
    for i in range(4):
        inverse.append(1.0 / work[i, i])
        for j in range(i + 1, 4):
            factor[i, j] = work[i, j] * inverse[i]
        for j in range(i + 1, 4):
            for k in range(j, 4):
                work[j, k] = work[j, k] - factor[i, j] * work[i, k]
            right[j] = right[j] - factor[i, j] * right[i]
    sol = [right[i] * inverse[i] for i in range(4)]
    for i in reversed(range(4)):
        for j in range(i):
            sol[j] = sol[j] - factor[j, i] * sol[i]
    res = [1.0 - rho * sol[0]]
    for i in range(1, 4):
        res.append(-(rho * sol[i] + theta * sol[i - 1]))
    res.append(-theta * sol[3])

    def wide(line):
        return jnp.concatenate([line] * 4, axis=1)

    for base, factors in ((0, sol), (160, res)):
        value = combine([(wide(c), x) for c, x in zip(factors, moved)])
        for c in range(4):
            out_ref[pl.ds(base + c, 40, stride=4), :] = value[:, LANES * c : LANES * (c + 1)]


def local(right_side, elem_faces, elem_class, elem_scale, stretch, pml_flag, send_faces, blocks):
    vmem = pl.BlockSpec(memory_space=pltpu.VMEM)
    fields = jax.ShapeDtypeStruct((320, LANES), F32)
    given = (right_side.reshape(160, LANES), elem_faces, elem_class, elem_scale, stretch, pml_flag, send_faces, blocks)
    both = pl.pallas_call(
        kernel,
        out_shape=fields,
        in_specs=[pl.BlockSpec(memory_space=pl.ANY)] * len(given),
        out_specs=vmem,
        scratch_shapes=[pltpu.VMEM(x.shape, x.dtype) for x in given]
        + [
            pltpu.VMEM((120, 640), F32),
            pltpu.VMEM((256, 1024), BF16),
            pltpu.VMEM((512, 896), BF16),
            pltpu.VMEM((896, 1024), BF16),
            pltpu.VMEM((1024, 896), BF16),
            pltpu.VMEM((1024, 512), F32),
            pltpu.VMEM((960, 512), BF16),
            pltpu.VMEM((320, 1024), BF16),
            pltpu.VMEM((960, LANES), F32),
            pltpu.VMEM((1024, 256), BF16),
            pltpu.VMEM((1024, 256), BF16),
            pltpu.VMEM((STEPS, 7, 40, LANES), F32),
            pltpu.VMEM((STEPS, 6, 40, LANES), F32),
            pltpu.VMEM((1, PLANE, 1, LANES), F32),
            pltpu.VMEM((1, N_GZ, 1, LANES), F32),
            pltpu.SemaphoreType.DMA((STEPS, 6)),
            pltpu.SemaphoreType.DMA((STEPS, 6)),
            pltpu.SemaphoreType.DMA((1,)),
            pltpu.SemaphoreType.DMA((1,)),
            pltpu.SemaphoreType.DMA((1,)),
            pltpu.SemaphoreType.DMA((1,)),
            pltpu.SemaphoreType.DMA((len(given),)),
            pltpu.SemaphoreType.REGULAR,
            pltpu.SemaphoreType.REGULAR,
        ],
        compiler_params=pltpu.CompilerParams(
            collective_id=0, has_side_effects=True, vmem_limit_bytes=40 * 1024 * 1024
        ),
    )(*[pltpu.with_memory_space_constraint(x, pltpu.HBM) for x in given])
    return both[:160].reshape(right_side.shape), both[160:].reshape(right_side.shape)


def solution(mesh):
    in_specs = (
        P(None, "gx", "gy", "gz"),
        P(None, "gx", "gy", "gz"),
        P("gx", "gy", "gz"),
        P("gx", "gy", "gz"),
        P(None, "gx", "gy", "gz"),
        P("gx", "gy", "gz"),
        P(None, "gx", "gy", "gz"),
        P(),
    )
    out_specs = (P(None, "gx", "gy", "gz"), P(None, "gx", "gy", "gz"))
    return jax.shard_map(local, mesh=mesh, in_specs=in_specs, out_specs=out_specs, check_vma=False)
```

```python
import functools

import jax
import jax.numpy as jnp
import numpy as np
from jax import lax
from jax.experimental import pallas as pl
from jax.experimental.pallas import tpu as pltpu
from jax.sharding import PartitionSpec as P

MESH = pl.DeviceIdType.MESH
F32 = jnp.float32
BF16 = jnp.bfloat16
N_GX, N_GY, N_GZ = 8, 4, 16
AXES = (("gx", N_GX), ("gy", N_GY), ("gz", N_GZ))
PLANE = N_GX * N_GY
LANES = 128
TILE = (0, 1, 2, 3, 5, 6)
STEPS = 5


def dot(a, b):
    return jnp.dot(a, b, preferred_element_type=F32)


def dot_nt(a, b):
    return lax.dot_general(a, b, (((1,), (1,)), ((), ())), preferred_element_type=F32)


def pieces(value, count):
    out = []
    for _ in range(count):
        head = value.astype(BF16).astype(F32)
        out.append(head)
        value = value - head
    return out


def onehot(left, right):
    return jnp.where(left == right, 1.0, 0.0).astype(BF16)


def embed_rows():
    column = lax.broadcasted_iota(jnp.int32, (1, 1024), 1)
    part, inside = column // 512, column % 512
    copy, place = inside // 160, inside % 160
    face, rest = place // 40, place % 40
    row = face * 20 + rest % 20 + jnp.where(copy == 2, 128, 0)
    return jnp.where((copy < 3) & (rest // 20 == part), row, -1)


def kernel(
    rhs_in,
    faces_in,
    class_in,
    scale_in,
    stretch_in,
    flag_in,
    send_in,
    blocks_in,
    out_ref,
    rhs_ref,
    faces_ref,
    class_ref,
    scale_ref,
    stretch_ref,
    flag_ref,
    send_ref,
    blocks_ref,
    lines640,
    embed,
    place,
    pick,
    pick_t,
    raw,
    smat,
    smat_t,
    rows,
    zhi,
    zlo,
    part,
    inbox,
    plane_buf,
    line_buf,
    halo_send,
    halo_recv,
    plane_send,
    plane_recv,
    line_send,
    line_recv,
    load_sem,
    near_sem,
    far_sem,
):
    at = {name: lax.axis_index(name) for name, _ in AXES}
    size = dict(AXES)

    def device(**moved):
        return tuple(moved.get(name, at[name]) for name, _ in AXES)

    neighbours, exists = [], []
    for name, n in AXES:
        neighbours.append(device(**{name: lax.rem(at[name] + (n - 1), n)}))
        neighbours.append(device(**{name: lax.rem(at[name] + 1, n)}))
        exists.append(at[name] > 0)
        exists.append(at[name] < n - 1)
    plane_at = at["gx"] * N_GY + at["gy"]
    offsets = [(dx, dy) for dx in range(N_GX) for dy in range(N_GY) if dx or dy]
    offsets.sort(key=lambda d: -(min(d[0], N_GX - d[0]) // 2 + min(d[1], N_GY - d[1])))
    plane_devices = []
    for dx, dy in offsets:
        plane_devices.append(device(gx=lax.rem(at["gx"] + dx, N_GX), gy=lax.rem(at["gy"] + dy, N_GY)))
    line_devices = []
    for step in sorted(range(1, N_GZ), key=lambda d: -min(d, N_GZ - d)):
        line_devices.append(device(gz=lax.rem(at["gz"] + step, N_GZ)))

    barrier = pltpu.get_barrier_semaphore()
    for other in reversed(neighbours):
        pl.semaphore_signal(barrier, inc=1, device_id=other, device_id_type=MESH)

    loads = []
    held = (send_ref, rhs_ref, faces_ref, blocks_ref, class_ref, scale_ref, stretch_ref, flag_ref)
    given = (send_in, rhs_in, faces_in, blocks_in, class_in, scale_in, stretch_in, flag_in)
    for i, (there, here) in enumerate(zip(given, held)):
        copy = pltpu.make_async_copy(there, here, load_sem.at[i])
        copy.start()
        loads.append(copy)

    def tell(sem, others):
        for other in others:
            pl.semaphore_signal(sem, inc=1, device_id=other, device_id_type=MESH)

    def along(name, *steps):
        return [device(**{name: lax.rem(at[name] + step, size[name])}) for step in steps]

    sends = []

    def send_halo(step, directions):
        for k in directions:
            copy = pltpu.make_async_remote_copy(
                src_ref=part.at[step, TILE[k]],
                dst_ref=inbox.at[step, k ^ 1],
                send_sem=halo_send.at[step, k],
                recv_sem=halo_recv.at[step, k ^ 1],
                device_id=neighbours[k],
                device_id_type=MESH,
            )
            copy.start()
            sends.append(copy)

    lane40 = lax.broadcasted_iota(jnp.int32, (40, LANES), 1)
    own_half = lane40 < 64

    def receive(step, k):
        pltpu.make_async_copy(inbox.at[step, k], inbox.at[step, k], halo_recv.at[step, k]).wait()
        mine, got = part[step, TILE[k]], pltpu.roll(inbox[step, k], 64, 1)
        return jnp.where(exists[k], mine + got, jnp.where(own_half, mine, 0.0))

    def start_sum(buf, send_sem, recv_sem, which, slot, others, value):
        buf[which, pl.ds(slot, 1)] = value[None]
        for other in others:
            pltpu.make_async_remote_copy(
                src_ref=buf.at[which, pl.ds(slot, 1)],
                dst_ref=buf.at[which, pl.ds(slot, 1)],
                send_sem=send_sem.at[which],
                recv_sem=recv_sem.at[which],
                device_id=other,
                device_id_type=MESH,
            ).start()

    def wait_all(buf, sem, which, count):
        some = buf.at[which, pl.ds(0, count)]
        pltpu.make_async_copy(some, some, sem.at[which]).wait()

    def start_plane(which, value):
        start_sum(plane_buf, plane_send, plane_recv, which, plane_at, plane_devices, value)

    def plane_to_line(which):
        wait_all(plane_buf, plane_recv, which, PLANE - 1)
        value = jnp.sum(plane_buf[which], axis=0)
        start_sum(line_buf, line_send, line_recv, which, at["gz"], line_devices, value)

    def finish_line(which):
        wait_all(line_buf, line_recv, which, N_GZ - 1)
        return jnp.sum(line_buf[which], axis=0)

    face512 = lax.broadcasted_iota(jnp.int32, (512, LANES), 0)
    no_face = jnp.full((1, 64), -1, jnp.int32)
    loads[0].wait()
    for k in range(6):
        shared = jnp.concatenate([send_ref[k, 0], no_face], axis=1)
        place[:, LANES * TILE[k] : LANES * (TILE[k] + 1)] = onehot(face512, shared)
    loads[1].wait()
    rhs = jnp.concatenate([rhs_ref[pl.ds(c, 40, stride=4), :] for c in range(4)], axis=1)
    rhs_split = jnp.concatenate(pieces(rhs, 3), axis=0).astype(BF16)

    def put(low, high):
        placed = dot(rhs_split, place[:, LANES * low : LANES * high])
        placed = placed[0:40] + placed[40:80] + placed[80:120]
        for t in range(low, high):
            part[0, t] = placed[:, LANES * (t - low) : LANES * (t - low + 1)]

    put(5, 7)
    put(0, 4)
    pl.semaphore_wait(barrier, 6)
    send_halo(0, (4, 5, 2, 3, 0, 1))

    position = lax.broadcasted_iota(jnp.int32, (1, 384), 1)
    target = ((position // 64) * 128 + jnp.where(position >= 256, 128, 0) + position % 64 + 1).astype(F32)
    face_col = lax.broadcasted_iota(jnp.int32, (512, 1), 0)
    sent = jnp.concatenate([send_ref[k, 0] for k in range(6)], axis=1)
    found = jnp.sum(jnp.where(face_col == sent, target, 0.0), axis=1, keepdims=True)
    inner = jnp.broadcast_to(jnp.where(found > 0.0, 0.0, 1.0), (512, LANES)).astype(BF16)
    below = jnp.where(
        lax.broadcasted_iota(jnp.int32, (512, 512), 1) < lax.broadcasted_iota(jnp.int32, (512, 512), 0), 1.0, 0.0
    ).astype(BF16)
    rank = dot(below, inner)
    new_place = jnp.where(jnp.broadcast_to(found, (512, LANES)) > 0.0, found - 1.0, 512.0 + rank)
    lane512 = lax.broadcasted_iota(jnp.int32, (512, LANES), 1)
    place[:, 512:640] = onehot(new_place.astype(jnp.int32), lane512 + 512)
    put(4, 5)

    place_row = new_place.T[0:8, :]
    high = jnp.floor(place_row * (1.0 / 32.0))
    digits = jnp.concatenate([high, place_row - 32.0 * high], axis=0).astype(BF16)
    row512 = lax.broadcasted_iota(jnp.int32, (512, 256), 0)
    row128 = lax.broadcasted_iota(jnp.int32, (LANES, 256), 0)
    lane256 = lax.broadcasted_iota(jnp.int32, (256, LANES), 1)
    loads[2].wait()
    for f in range(4):
        old = faces_ref[f, 0]
        looked = dot(digits, onehot(row512, old))
        owned = (looked[0:1] * 32.0 + looked[8:9]).astype(jnp.int32)
        slot = old - 512
        new = jnp.where(old < 512, owned, (slot // 64) * 128 + jnp.where(slot >= 256, 128, 0) + 64 + slot % 64)
        for t in range(7):
            pick[LANES * t : LANES * (t + 1), 256 * f : 256 * (f + 1)] = onehot(row128 + LANES * t, new)
        column = jnp.broadcast_to(new.astype(F32), (LANES, 256)).T.astype(jnp.int32)
        for t in range(7):
            pick_t[256 * f : 256 * (f + 1), LANES * t : LANES * (t + 1)] = onehot(column, lane256 + LANES * t)

    embed[...] = onehot(lax.broadcasted_iota(jnp.int32, (256, 1024), 0), embed_rows())
    loads[3].wait()
    for b in range(6):
        for g in range(10):
            lines640[20 * b + 2 * g : 20 * b + 2 * g + 2, :] = blocks_ref[b // 3, b % 3, :, 640 * g : 640 * g + 640]
    for k in range(8):
        piece = lines640[:, 80 * k : 80 * k + 80]
        rows[pl.ds(k, 120, stride=8), :] = jnp.concatenate([piece, jnp.zeros((120, 48), F32)], axis=1)
    for b in range(6):
        both = jnp.concatenate(pieces(rows[160 * b : 160 * b + 160, :], 2), axis=1).astype(BF16)
        spread = dot(both, embed[...]).reshape(10, 2, 8, 1024)
        real, imag = spread[:, 0].reshape(80, 1024), spread[:, 1].reshape(80, 1024)
        block = jnp.concatenate([real[:, :512] - imag[:, 512:], imag[:, :512] + real[:, 512:]], axis=0)
        raw[160 * b : 160 * b + 160, :] = block
        smat[160 * b : 160 * b + 160, :] = block.astype(BF16)
    raw[960:1024, :] = jnp.zeros((64, 512), F32)
    smat_t[0:160, :] = raw[:, 0:256].T[0:160].astype(BF16)
    smat_t[160:320, :] = raw[:, 256:512].T[64:224].astype(BF16)
    zhi[960:1024, :] = jnp.zeros((64, 256), BF16)
    zlo[960:1024, :] = jnp.zeros((64, 256), BF16)
    for copy in loads[4:]:
        copy.wait()
    weights = []
    for c in range(2):
        for d in range(3):
            factor = jnp.where(flag_ref[0] > 0, stretch_ref[d, 0], 1.0)
            weights.append(jnp.where(class_ref[0] == c, scale_ref[0] * factor, 0.0))

    def gather(tiles, low, high):
        split = pieces(jnp.concatenate(tiles, axis=1), 2)
        return dot(jnp.concatenate(split, axis=0).astype(BF16), pick[low:high, :])

    def project(picked, with_energy):
        upper = [picked[0:40, 256 * f : 256 * f + 256] for f in range(4)]
        lower = [picked[40:80, 256 * f : 256 * f + 256] for f in range(4)]
        stacked = jnp.concatenate(upper + lower + upper + [jnp.zeros((32, 256), F32)], axis=0).astype(BF16)
        energy = jnp.zeros((8, 256), F32)
        for b in range(6):
            projected = dot(smat[160 * b : 160 * b + 160, :], stacked)
            weighted = projected * weights[b]
            if with_energy:
                energy = energy + jnp.sum((weighted * projected).reshape(20, 8, 256), axis=0)
            head, tail = pieces(weighted, 2)
            zhi[160 * b : 160 * b + 160, :] = head.astype(BF16)
            zlo[160 * b : 160 * b + 160, :] = tail.astype(BF16)
        return energy

    def scatter(step):
        both = dot(smat_t[...], zhi[...])
        image = both[0:160] + both[160:320] + dot(smat_t[0:160, :], zlo[...])
        wide = jnp.concatenate([image[40 * f : 40 * f + 40] for f in range(4)], axis=1)
        split = jnp.concatenate(pieces(wide, 3), axis=0).astype(BF16)
        for tiles, directions in (((5, 6), (4, 5)), ((2, 3), (2, 3)), ((0, 1), (0, 1)), ((4,), ())):
            low = LANES * tiles[0]
            spread = dot(split, pick_t[:, low : low + LANES * len(tiles)])
            spread = spread[0:40] + spread[40:80] + spread[80:120]
            for n, t in enumerate(tiles):
                part[step, t] = spread[:, LANES * n : LANES * (n + 1)]
            send_halo(step, directions)

    def own(tiles):
        return [x if t == 4 else jnp.where(own_half, x, 0.0) for t, x in enumerate(tiles)]

    def product(mine, tiles):
        total = mine[0] * tiles[0]
        for t in range(1, 7):
            total = total + mine[t] * tiles[t]
        return jnp.sum(total, axis=0, keepdims=True)

    def energy_row(energy):
        row = jnp.sum(energy, axis=0, keepdims=True)
        return row[:, 0:128] + row[:, 128:256]

    def to_lanes(lines):
        square = jnp.concatenate(lines + [jnp.zeros((16 - len(lines), LANES), F32)], axis=0)
        sums = jnp.sum(square, axis=1, keepdims=True)
        on_diagonal = lax.broadcasted_iota(jnp.int32, (16, LANES), 0) == lax.broadcasted_iota(jnp.int32, (16, LANES), 1)
        return jnp.sum(jnp.where(on_diagonal, sums, 0.0), axis=0, keepdims=True)

    def scalar(line, q):
        return jnp.broadcast_to(line[:, q : q + 1], (1, LANES))

    def combine(terms):
        total = None
        for factor, value in terms:
            total = factor * value if total is None else total + factor * value
        return total

    def back(tiles_list):
        stack = []
        for tiles in tiles_list:
            stack += pieces(jnp.concatenate(tiles, axis=1), 3)
        moved = dot_nt(jnp.concatenate(stack, axis=0).astype(BF16), place[...])
        out = []
        for i in range(len(tiles_list)):
            out.append(moved[120 * i : 120 * i + 40] + moved[120 * i + 40 : 120 * i + 80] + moved[120 * i + 80 : 120 * i + 120])
        return out

    total = blocks_ref[...]
    total = jnp.sum(total * total, axis=(0, 1, 2))
    rho = 1.0 + jnp.sum(total.reshape(1, 6400), axis=1, keepdims=True) * (3.0 / 160.0)
    rho = jnp.broadcast_to(rho, (1, LANES))
    theta = 256.0 * rho
    inv_theta = 1.0 / theta
    keep = (1.0 - rho) * inv_theta

    basis, masked, sums, moved = [], [], {}, [rhs]

    def advance(step):
        def tile(t, got):
            return got if step == 0 else keep * basis[-1][t] + inv_theta * got

        tiles = {4: tile(4, part[step, 4])}
        picked = gather([tiles[4]], 512, 640) if step < 4 else None
        for pair in ((0, 1), (2, 3), (4, 5)):
            for k in pair:
                tiles[TILE[k]] = tile(TILE[k], receive(step, k))
            if step < 4:
                low, high = TILE[pair[0]], TILE[pair[1]]
                picked = picked + gather([tiles[low], tiles[high]], LANES * low, LANES * (high + 1))
        basis.append([tiles[t] for t in range(7)])
        return picked

    def add_inner(i, j):
        sums[i, j] = product(masked[i], basis[j])

    for step in range(3):
        if step == 1:
            pl.semaphore_wait(near_sem, 4)
            tell(far_sem, along("gz", 4, 12) + along("gy", 1, 2, 3))
        picked = advance(step)
        if step == 0:
            tell(near_sem, along("gz", 2, 14) + along("gx", 2, 6))
        project(picked, False)
        masked.append(own(basis[step]))
        scatter(step + 1)
        for i in range(step + 1):
            add_inner(i, step)
        if step:
            moved += back([basis[step]])
    picked = advance(3)
    pl.semaphore_wait(far_sem, 5)
    masked.append(own(basis[3]))
    for i in range(4):
        add_inner(i, 3)
    pairs = [(i, j) for i in range(4) for j in range(i, 4)]
    products = to_lanes([sums[pair] for pair in pairs] + [sums[3, 3]])
    energy = jnp.sum(energy_row(project(picked, True)), axis=1, keepdims=True)
    lane = lax.broadcasted_iota(jnp.int32, (1, LANES), 1)
    start_plane(0, products + jnp.where(lane == len(pairs), energy, 0.0))
    scatter(4)
    plane_to_line(0)
    moved += back([basis[3]])
    advance(4)
    moved += back([basis[4]])
    for copy in sends:
        copy.wait_send()
    wait_all(plane_buf, plane_send, 0, PLANE - 1)
    wait_all(line_buf, line_send, 0, N_GZ - 1)
    totals = finish_line(0)

    gram = {}
    for q, (i, j) in enumerate(pairs):
        gram[i, j] = gram[j, i] = scalar(totals, q)
    gram[3, 4] = (scalar(totals, len(pairs)) - rho * gram[3, 3]) * inv_theta
    gram[2, 4] = gram[3, 3]
    gram[1, 4] = gram[2, 3]
    gram[0, 4] = gram[1, 3]

    work = {(i, j): theta * gram[i, j + 1] + rho * gram[i, j] for i, j in pairs}
    right = [gram[0, i] for i in range(4)]
    factor, inverse = {}, []
    for i in range(4):
        inverse.append(1.0 / work[i, i])
        for j in range(i + 1, 4):
            factor[i, j] = work[i, j] * inverse[i]
        for j in range(i + 1, 4):
            for k in range(j, 4):
                work[j, k] = work[j, k] - factor[i, j] * work[i, k]
            right[j] = right[j] - factor[i, j] * right[i]
    sol = [right[i] * inverse[i] for i in range(4)]
    for i in reversed(range(4)):
        for j in range(i):
            sol[j] = sol[j] - factor[j, i] * sol[i]
    res = [1.0 - rho * sol[0]]
    for i in range(1, 4):
        res.append(-(rho * sol[i] + theta * sol[i - 1]))
    res.append(-theta * sol[3])

    def wide(line):
        return jnp.concatenate([line] * 4, axis=1)

    for base, factors in ((0, sol), (160, res)):
        value = combine([(wide(c), x) for c, x in zip(factors, moved)])
        for c in range(4):
            out_ref[pl.ds(base + c, 40, stride=4), :] = value[:, LANES * c : LANES * (c + 1)]


def local(right_side, elem_faces, elem_class, elem_scale, stretch, pml_flag, send_faces, blocks):
    vmem = pl.BlockSpec(memory_space=pltpu.VMEM)
    fields = jax.ShapeDtypeStruct((320, LANES), F32)
    given = (right_side.reshape(160, LANES), elem_faces, elem_class, elem_scale, stretch, pml_flag, send_faces, blocks)
    both = pl.pallas_call(
        kernel,
        out_shape=fields,
        in_specs=[pl.BlockSpec(memory_space=pl.ANY)] * len(given),
        out_specs=vmem,
        scratch_shapes=[pltpu.VMEM(x.shape, x.dtype) for x in given]
        + [
            pltpu.VMEM((120, 640), F32),
            pltpu.VMEM((256, 1024), BF16),
            pltpu.VMEM((512, 896), BF16),
            pltpu.VMEM((896, 1024), BF16),
            pltpu.VMEM((1024, 896), BF16),
            pltpu.VMEM((1024, 512), F32),
            pltpu.VMEM((960, 512), BF16),
            pltpu.VMEM((320, 1024), BF16),
            pltpu.VMEM((960, LANES), F32),
            pltpu.VMEM((1024, 256), BF16),
            pltpu.VMEM((1024, 256), BF16),
            pltpu.VMEM((STEPS, 7, 40, LANES), F32),
            pltpu.VMEM((STEPS, 6, 40, LANES), F32),
            pltpu.VMEM((1, PLANE, 1, LANES), F32),
            pltpu.VMEM((1, N_GZ, 1, LANES), F32),
            pltpu.SemaphoreType.DMA((STEPS, 6)),
            pltpu.SemaphoreType.DMA((STEPS, 6)),
            pltpu.SemaphoreType.DMA((1,)),
            pltpu.SemaphoreType.DMA((1,)),
            pltpu.SemaphoreType.DMA((1,)),
            pltpu.SemaphoreType.DMA((1,)),
            pltpu.SemaphoreType.DMA((len(given),)),
            pltpu.SemaphoreType.REGULAR,
            pltpu.SemaphoreType.REGULAR,
        ],
        compiler_params=pltpu.CompilerParams(
            collective_id=0, has_side_effects=True, vmem_limit_bytes=40 * 1024 * 1024
        ),
    )(*[pltpu.with_memory_space_constraint(x, pltpu.HBM) for x in given])
    return both[:160].reshape(right_side.shape), both[160:].reshape(right_side.shape)


def solution(mesh):
    in_specs = (
        P(None, "gx", "gy", "gz"),
        P(None, "gx", "gy", "gz"),
        P("gx", "gy", "gz"),
        P("gx", "gy", "gz"),
        P(None, "gx", "gy", "gz"),
        P("gx", "gy", "gz"),
        P(None, "gx", "gy", "gz"),
        P(),
    )
    out_specs = (P(None, "gx", "gy", "gz"), P(None, "gx", "gy", "gz"))
    return jax.shard_map(local, mesh=mesh, in_specs=in_specs, out_specs=out_specs, check_vma=False)
```
